256 devices in a mesh: grp: 4 (over z_lo), seq: 64 (over x, y, z_hi, core).
Axes of the slice: x: 4, y: 4, z: 8 (z_hi: 2, z_lo: 4; z = z_hi * 4 + z_lo), core: 2. Of those that a mesh axis runs over, the one named last changes fastest.
Arguments:
- main_query: bfloat16 [64, 128, 2560], P('seq', 'grp'), may hold values from -150 to 150
- main_key: bfloat16 [64, 128, 2560], P('seq', 'grp'), may hold values from -4 to 4
- main_value: bfloat16 [64, 128, 2560], P('seq', 'grp'), may hold values from -240 to 240
- guide_query: bfloat16 [64, 128, 1024], P('seq', None, 'grp'), may hold values from -150 to 150
- guide_key: bfloat16 [64, 128, 1024], P('seq', None, 'grp'), may hold values from -4 to 4
- guide_value: bfloat16 [64, 128, 1024], P('seq', None, 'grp'), may hold values from -240 to 240
- latents: float32 [64, 128, 64], P('seq', 'grp'), may hold values from -6 to 6
- step_index: int32 [1], replicated, may hold values from 0 to 49
- main_mod: bfloat16 [50, 2, 2560], replicated, may hold values from -3 to 3
- guide_mod: bfloat16 [50, 2, 1024], replicated, may hold values from -3 to 3
- main_head: bfloat16 [2560, 64], replicated, may hold values from -0.125 to 0.125
- guide_head: bfloat16 [1024, 64], replicated, may hold values from -0.1875 to 0.1875
Outputs:
- velocity: float32 [64, 128, 64], P('seq', 'grp')
- next_latents: float32 [64, 128, 64], P('seq', 'grp')
The draws below stay inside these ranges and needn't reach their ends.
All inputs are finite; a program needn't handle non-finite values.
Results may differ from the reference program's by a relative error of at most 0.012.
Values may be sent and summed in bfloat16 or wider, within the bound.
No kernel may reach another device: no remote copies, remote signals or barrier semaphores. Data moves between devices by JAX's collectives and lax.ppermute only.
A program may use at most 128 MiB of HBM per device.

```python
import math
import jax
import jax.numpy as jnp
from jax import lax

HM = 20
HG = 8
C = 64
STEPS = 50
QM = 2560
QG = 1024
BLOCK = 128
BLOCKS = 64
TOKENS = 8192


def paired_rows(key, salt, width):
    seeded = jax.random.fold_in(key, salt)
    keys_base = jax.random.truncated_normal(jax.random.fold_in(seeded, 1), -4.0, 4.0, (TOKENS, width), jnp.float32)
    queries_base = jax.random.truncated_normal(jax.random.fold_in(seeded, 2), -4.0, 4.0, (TOKENS, width), jnp.float32)
    aligned = jax.random.randint(jax.random.fold_in(seeded, 3), (6,), 0, TOKENS)
    sources = jax.random.randint(jax.random.fold_in(seeded, 4), (6,), 0, TOKENS)
    copies = (sources + 1 + jax.random.randint(jax.random.fold_in(seeded, 5), (6,), 0, TOKENS - 1)) % TOKENS
    queries = queries_base.at[aligned].set(queries_base[aligned])
    keys = keys_base.at[copies].set(keys_base[copies])
    return (queries, keys)


def value_rows(seeded, width, row_spread):
    base = jax.random.truncated_normal(jax.random.fold_in(seeded, 1), -4.0, 4.0, (TOKENS, width), jnp.float32)
    ramp = 3.0 ** (jnp.arange(width, dtype=jnp.float32) / (width - 1))
    column_scale = 3.3 ** jax.random.uniform(jax.random.fold_in(seeded, 2), (width,), jnp.float32)
    row_scale = row_spread ** jax.random.uniform(jax.random.fold_in(seeded, 3), (TOKENS,), jnp.float32)
    return base * ramp[None, :] * column_scale[None, :] * row_scale[:, None]


def draw_main_query(key, part):
    drawn = paired_rows(key, 31, QM)
    return drawn[0].reshape(BLOCKS, BLOCK, QM).astype(jnp.bfloat16)


def draw_main_key(key, part):
    drawn = paired_rows(key, 31, QM)
    return drawn[1].reshape(BLOCKS, BLOCK, QM).astype(jnp.bfloat16)


def draw_guide_query(key, part):
    drawn = paired_rows(key, 47, QG)
    return drawn[0].reshape(BLOCKS, BLOCK, QG).astype(jnp.bfloat16)


def draw_guide_key(key, part):
    drawn = paired_rows(key, 47, QG)
    return drawn[1].reshape(BLOCKS, BLOCK, QG).astype(jnp.bfloat16)


def draw_main_value(key, part):
    key = jax.random.fold_in(key, 7)
    values = value_rows(key, QM, 1.0)
    return values.reshape(BLOCKS, BLOCK, QM).astype(jnp.bfloat16)


def draw_guide_value(key, part):
    key = jax.random.fold_in(key, 9)
    values = value_rows(key, QG, 1.0)
    return values.reshape(BLOCKS, BLOCK, QG).astype(jnp.bfloat16)


def levels(stream_key, extent, pieces, smallest, largest):
    level = 1.0
    for position, parts in pieces:
        draws = jax.random.uniform(jax.random.fold_in(jax.random.fold_in(stream_key, 6), position), (parts,), jnp.float32, smallest / len(pieces), largest / len(pieces))
        level = level * jnp.repeat(jnp.exp(draws), extent[position] // parts).reshape((-1,) + (1,) * (len(extent) - 1 - position))
    return level


def gaussian(stream_key, dims, scale, reach, pieces=(), kind=jnp.bfloat16):
    loudness = levels(stream_key, dims, pieces, -0.22, 0.18) if pieces else 1.0
    values = jax.random.normal(stream_key, dims, jnp.float32) * scale * loudness
    return jnp.minimum(jnp.maximum(values, -reach), reach).astype(kind)


def setup_inputs(seed: int = 0) -> dict:
    key_of = jax.random.split(jax.random.key(seed), 13)
    main_query = draw_main_query(jax.random.fold_in(key_of[12], 71), 0)
    main_key = draw_main_key(jax.random.fold_in(key_of[12], 71), 0)
    main_value = draw_main_value(jax.random.fold_in(key_of[12], 71), 0)
    guide_query = draw_guide_query(jax.random.fold_in(key_of[12], 71), 0)
    guide_key = draw_guide_key(jax.random.fold_in(key_of[12], 71), 0)
    guide_value = draw_guide_value(jax.random.fold_in(key_of[12], 71), 0)
    latents = gaussian(key_of[6], (BLOCKS, BLOCK, C), 1.0, 6.0, ((0, 64), (1, 4)), jnp.float32)
    step_index = jax.random.randint(key_of[7], (1,), 0, STEPS).astype(jnp.int32)
    main_mod = gaussian(key_of[8], (STEPS, 2, QM), 0.5, 3.0)
    guide_mod = gaussian(key_of[9], (STEPS, 2, QG), 0.5, 3.0)
    main_head = gaussian(key_of[10], (QM, C), QM ** -0.5, 0.125)
    guide_head = gaussian(key_of[11], (QG, C), QG ** -0.5, 0.1875)
    return dict(main_query=main_query, main_key=main_key, main_value=main_value, guide_query=guide_query, guide_key=guide_key, guide_value=guide_value, latents=latents, step_index=step_index, main_mod=main_mod, guide_mod=guide_mod, main_head=main_head, guide_head=guide_head)


guidance = 2.5
flow_shift = 3.0
epsilon = 1e-06

def attend(queries, keys, values, heads):
    total = queries.shape[0]
    width = queries.shape[1]
    depth = width // heads
    keys_wide = keys.astype(jnp.float32).reshape(total, heads, depth)
    values_wide = values.astype(jnp.float32).reshape(total, heads, depth)
    block = math.gcd(total, 512)
    grouped = queries.astype(jnp.float32).reshape(total // block, block, heads, depth)
    factor = 1.0 / math.sqrt(depth)

    def one_block(rows_here):
        scores = jnp.einsum('rhd,khd->hrk', rows_here, keys_wide) * factor
        highest = lax.optimization_barrier(jnp.max(scores, axis=-1, keepdims=True))
        weights = jnp.exp(scores - highest)
        weight_sum = lax.optimization_barrier(jnp.sum(weights, axis=-1))
        rounded = lax.optimization_barrier(weights.astype(jnp.bfloat16)).astype(jnp.float32)
        summed = jnp.einsum('hrk,khd->rhd', rounded, values_wide)
        return summed / jnp.transpose(weight_sum)[:, :, None]
    result = lax.map(one_block, grouped)
    return lax.optimization_barrier(result.reshape(total, width).astype(jnp.bfloat16))

def project(attended, table, step_now, weight):
    row_now = lax.dynamic_index_in_dim(table, step_now, 0, keepdims=False).astype(jnp.float32)
    values = attended.astype(jnp.float32)
    center = lax.optimization_barrier(jnp.mean(values, axis=-1, keepdims=True))
    centered = values - center
    spread = lax.optimization_barrier(jnp.mean(centered * centered, axis=-1, keepdims=True))
    normed = centered * lax.rsqrt(spread + epsilon)
    modulated = normed * (1.0 + row_now[1]) + row_now[0]
    return jnp.dot(modulated, weight.astype(jnp.float32), precision=lax.Precision.HIGHEST)

def sigma_at(index):
    remaining = 1.0 - index.astype(jnp.float32) / STEPS
    return flow_shift * remaining / (1.0 + (flow_shift - 1.0) * remaining)

def reference(main_query, main_key, main_value, guide_query, guide_key, guide_value, latents, step_index, main_mod, guide_mod, main_head, guide_head):
    step_now = step_index[0]
    main_out = attend(main_query.reshape(TOKENS, QM), main_key.reshape(TOKENS, QM), main_value.reshape(TOKENS, QM), HM)
    guide_out = attend(guide_query.reshape(TOKENS, QG), guide_key.reshape(TOKENS, QG), guide_value.reshape(TOKENS, QG), HG)
    main_flow = project(main_out, main_mod, step_now, main_head)
    guide_flow = project(guide_out, guide_mod, step_now, guide_head)
    velocity = (guide_flow + guidance * (main_flow - guide_flow)).reshape(latents.shape)
    advanced = latents + (sigma_at(step_now + 1) - sigma_at(step_now)) * velocity
    return (velocity, advanced)
```

```python
import math

import jax
import jax.numpy as jnp
from jax import lax
from jax.experimental import pallas as pl
from jax.experimental.pallas import tpu as pltpu
from jax.sharding import Mesh, PartitionSpec as P

HD = 128
STEPS = 50
ZL, X, Y, ZH, CORE = 4, 4, 4, 2, 2
Z = ZL * ZH
ROWS = 32
TOKENS = ROWS * Z
BLOCK = 128
FULL = 3
HALF = TOKENS // 2
QROWS = FULL * TOKENS + HALF
STAT = 32
OROWS = QROWS + STAT
PIECES = Y * CORE
KEYS = PIECES * TOKENS

guidance = 2.5
flow_shift = 3.0
epsilon = 1e-06
score_scale = math.log2(math.e) / math.sqrt(HD)

f32 = jnp.float32
bf16 = jnp.bfloat16
VMEM = pl.BlockSpec(memory_space=pltpu.VMEM)
SMEM = pl.BlockSpec(memory_space=pltpu.SMEM)


def params(mib):
    return pltpu.CompilerParams(vmem_limit_bytes=mib * 1024 * 1024)


def head_of(zh, zl, slot):
    return zl * 5 + (4 if slot == 2 else 2 * zh + slot)


def pack_kernel(half, mq, mk, mv, gq, gk, gv, send, guide_send, guide_own):
    zh = half[0]
    for zh_to in range(ZH):
        for zl_to in range(ZL):
            to = zh_to * ZL + zl_to
            for kind, ref in enumerate((mq, mk, mv)):
                for slot in range(3):
                    head = head_of(zh_to, zl_to, slot)
                    send[to, kind * 3 + slot] = ref[0, :, head * HD : (head + 1) * HD]
    own = pl.ds(pl.multiple_of(zh * HD, HD), HD)
    other = pl.ds(pl.multiple_of((1 - zh) * HD, HD), HD)
    for kind, ref in enumerate((gq, gk, gv)):
        guide_own[kind] = ref[0, :, own]
        guide_send[kind] = ref[0, :, other]


def unpack_kernel(half, got, guide_own, guide_got, queries, pairs):
    zh = half[0]
    for source in range(Z):
        rows = pl.ds(source * ROWS, ROWS)
        for slot in range(2):
            queries[pl.ds(slot * TOKENS + source * ROWS, ROWS), :] = got[source, slot]
        for kind in range(2):
            for slot, place in ((0, 0), (1, 1), (2, 3)):
                pairs[kind * 4 + place, rows, :] = got[source, (kind + 1) * 3 + slot]
    for zl in range(ZL):
        queries[pl.ds(FULL * TOKENS + zl * ROWS, ROWS), :] = got[zh * ZL + zl, 2]
    for ref, place in ((guide_own, zh), (guide_got, 1 - zh)):
        at = pl.multiple_of(place * BLOCK, BLOCK)
        queries[pl.ds(2 * TOKENS + at, BLOCK), :] = ref[0]
        pairs[2, pl.ds(at, BLOCK), :] = ref[1]
        pairs[6, pl.ds(at, BLOCK), :] = ref[2]


def diagonal():
    return lax.broadcasted_iota(jnp.int32, (HD, HD), 0) == lax.broadcasted_iota(
        jnp.int32, (HD, HD), 1
    )


def attend_kernel(*refs):
    queries, pairs = refs[:X], refs[X : X + PIECES]
    outs = refs[X + PIECES : 2 * X + PIECES]
    keys, values, scores, weights, stats = refs[2 * X + PIECES :]
    for piece in range(PIECES):
        rows = pl.ds(piece * TOKENS, TOKENS)
        for head in range(4):
            keys[head, rows, :] = pairs[piece][head]
            values[head, rows, :HD] = pairs[piece][4 + head]
            values[head, rows, HD:] = jnp.ones((TOKENS, HD), bf16)
    on_diagonal = diagonal()

    def score_tile(place, query, head):
        size = query.shape[0]
        highest = None
        for piece in range(PIECES):
            part = lax.dot_general(
                query,
                keys[head, pl.ds(piece * TOKENS, TOKENS), :],
                (((1,), (1,)), ((), ())),
                preferred_element_type=f32,
            )
            scores[place, :size, pl.ds(piece * TOKENS, TOKENS)] = part
            here = jnp.maximum(part[:, :HD], part[:, HD:])
            highest = here if highest is None else jnp.maximum(highest, here)
        return jnp.max(highest, axis=1, keepdims=True) * score_scale

    def weight_tile(place, size, highest, head):
        for piece in range(PIECES):
            columns = pl.ds(piece * TOKENS, TOKENS)
            part = scores[place, :size, columns]
            weights[place, :size, columns] = jnp.exp2(part * score_scale - highest).astype(bf16)
        return jnp.dot(weights[place, :size, :], values[head], preferred_element_type=f32)

    def store_tile(source, start, size, highest, total, first_stat):
        weight_sum = total[:, HD:]
        outs[source][pl.ds(start, size), :] = (total[:, :HD] / weight_sum).astype(bf16)
        level = highest + jnp.log2(weight_sum)
        for part in range(size // HD):
            block = level[part * HD : (part + 1) * HD, :]
            row = jnp.sum(jnp.where(on_diagonal, block, 0.0), axis=0, keepdims=True)
            stats[source, pl.ds(first_stat + part, 1), :] = row

    def full_head(head, carry):
        start = pl.multiple_of(head * TOKENS, TOKENS)
        tops = [
            score_tile(source, queries[source][pl.ds(start, TOKENS), :], head)
            for source in range(X)
        ]
        for source in range(X):
            total = weight_tile(source, TOKENS, tops[source], head)
            store_tile(source, start, TOKENS, tops[source], total, head * 2)
        return carry

    stats[...] = jnp.zeros_like(stats)
    lax.fori_loop(0, FULL, full_head, 0)
    tops = [
        score_tile(source, queries[source][FULL * TOKENS :, :], FULL) for source in range(X)
    ]
    for source in range(X):
        total = weight_tile(source, HALF, tops[source], FULL)
        store_tile(source, FULL * TOKENS, HALF, tops[source], total, FULL * 2)
    for source in range(X):
        level = stats[source]
        high = level.astype(bf16).astype(f32)
        middle = (level - high).astype(bf16).astype(f32)
        low = level - high - middle
        block = jnp.concatenate([high, middle, low, jnp.zeros_like(low)], axis=0)
        outs[source][QROWS:, :] = block.astype(bf16)


def combine_kernel(*refs):
    parts, send = refs[:X], refs[X]
    on_diagonal = diagonal()
    levels = []
    for part in parts:
        block = part[QROWS:, :].astype(f32)
        levels.append(block[0:8] + block[8:16] + block[16:24])
    top = levels[0]
    for level in levels[1:]:
        top = jnp.maximum(top, level)
    shares = [jnp.exp2(level - top) for level in levels]
    whole = shares[0] + shares[1] + shares[2] + shares[3]
    shares = [share / whole for share in shares]
    for tile in range(QROWS // HD):
        total = None
        for part, share in zip(parts, shares):
            row = jnp.broadcast_to(share[tile : tile + 1, :], (HD, HD))
            column = jnp.sum(jnp.where(on_diagonal, row, 0.0), axis=1, keepdims=True)
            term = part[tile * HD : (tile + 1) * HD, :].astype(f32) * column
            total = term if total is None else total + term
        result = total.astype(bf16)
        for zl in range(ZL):
            rows = result[zl * ROWS : (zl + 1) * ROWS, :]
            if tile < FULL * 2:
                slot = (0, 1, 3)[tile // 2]
                send[(tile % 2) * ZL + zl, slot] = rows
            else:
                send[zl, 2] = rows
                send[ZL + zl, 2] = rows


def split_dot(left, weight):
    high = left.astype(bf16)
    low = (left - high.astype(f32)).astype(bf16)
    return jnp.dot(high, weight, preferred_element_type=f32) + jnp.dot(
        low, weight, preferred_element_type=f32
    )


def flow_of(heads, table, weight):
    width = len(heads) * HD
    center = sum(jnp.sum(h, axis=1, keepdims=True) for h in heads) / width
    centered = [h - center for h in heads]
    spread = sum(jnp.sum(h * h, axis=1, keepdims=True) for h in centered) / width
    shrink = lax.rsqrt(spread + epsilon)
    shift, scale = table[0, 0:1, :].astype(f32), table[0, 1:2, :].astype(f32)
    total = None
    for index, head in enumerate(centered):
        lanes = slice(index * HD, (index + 1) * HD)
        modulated = head * shrink * (1.0 + scale[:, lanes]) + shift[:, lanes]
        term = split_dot(modulated, weight[lanes, :])
        total = term if total is None else total + term
    return total


def sigma_at(index):
    remaining = 1.0 - index.astype(f32) / STEPS
    return flow_shift * remaining / (1.0 + (flow_shift - 1.0) * remaining)


def final_kernel(
    step, half, got, latents, main_mod, guide_mod, main_head, guide_head, velocity, advanced
):
    zh = half[0]
    main, guide = [], []
    for zl in range(ZL):
        main += [got[0 * ZL + zl, 0], got[0 * ZL + zl, 1]]
        main += [got[1 * ZL + zl, 0], got[1 * ZL + zl, 1]]
        main += [got[zh * ZL + zl, 2]]
        guide += [got[0 * ZL + zl, 3], got[1 * ZL + zl, 3]]
    main_flow = flow_of([h.astype(f32) for h in main], main_mod, main_head)
    guide_flow = flow_of([h.astype(f32) for h in guide], guide_mod, guide_head)
    result = guide_flow + guidance * (main_flow - guide_flow)
    now = jnp.full((1, 1), step[0], jnp.int32)
    velocity[0] = result
    advanced[0] = latents[0] + (sigma_at(now + 1) - sigma_at(now)) * result


def shifted(array, axis, size, by):
    return lax.ppermute(array, axis, [(i, (i + by) % size) for i in range(size)])


def on_device(
    main_query,
    main_key,
    main_value,
    guide_query,
    guide_key,
    guide_value,
    latents,
    step_index,
    main_mod,
    guide_mod,
    main_head,
    guide_head,
):
    half = lax.axis_index("zh").astype(jnp.int32).reshape(1)
    send, guide_send, guide_own = pl.pallas_call(
        pack_kernel,
        out_shape=(
            jax.ShapeDtypeStruct((Z, 9, ROWS, HD), bf16),
            jax.ShapeDtypeStruct((3, BLOCK, HD), bf16),
            jax.ShapeDtypeStruct((3, BLOCK, HD), bf16),
        ),
        in_specs=[SMEM] + [VMEM] * 6,
        out_specs=(VMEM,) * 3,
        compiler_params=params(16),
        name="pack",
    )(half, main_query, main_key, main_value, guide_query, guide_key, guide_value)
    guide_got = shifted(guide_send, "zh", ZH, 1)
    got = lax.all_to_all(send, ("zh", "zl"), split_axis=0, concat_axis=0, tiled=True)
    queries, pairs = pl.pallas_call(
        unpack_kernel,
        out_shape=(
            jax.ShapeDtypeStruct((QROWS, HD), bf16),
            jax.ShapeDtypeStruct((8, TOKENS, HD), bf16),
        ),
        in_specs=[SMEM] + [VMEM] * 3,
        out_specs=(VMEM,) * 2,
        compiler_params=params(16),
        name="unpack",
    )(half, got, guide_own, guide_got)

    own_pairs = [pairs] + [shifted(pairs, "y", Y, by) for by in (1, -1, 2)]
    all_queries = [queries] + [shifted(queries, "x", X, by) for by in (1, -1, 2)]
    all_pairs = own_pairs + [shifted(p, "core", CORE, 1) for p in own_pairs]
    parts = pl.pallas_call(
        attend_kernel,
        out_shape=(jax.ShapeDtypeStruct((OROWS, HD), bf16),) * X,
        in_specs=[VMEM] * (X + PIECES),
        out_specs=(VMEM,) * X,
        scratch_shapes=[
            pltpu.VMEM((4, KEYS, HD), bf16),
            pltpu.VMEM((4, KEYS, 2 * HD), bf16),
            pltpu.VMEM((X, TOKENS, KEYS), f32),
            pltpu.VMEM((X, TOKENS, KEYS), bf16),
            pltpu.VMEM((X, 8, HD), f32),
        ],
        compiler_params=params(48),
        name="attend",
    )(*all_queries, *all_pairs)
    back = [parts[0]] + [shifted(p, "x", X, -by) for p, by in zip(parts[1:], (1, -1, 2))]
    send = pl.pallas_call(
        combine_kernel,
        out_shape=jax.ShapeDtypeStruct((Z, 4, ROWS, HD), bf16),
        in_specs=[VMEM] * X,
        out_specs=VMEM,
        compiler_params=params(16),
        name="combine",
    )(*back)
    got = lax.all_to_all(send, ("zh", "zl"), split_axis=0, concat_axis=0, tiled=True)
    grid_spec = pltpu.PrefetchScalarGridSpec(
        num_scalar_prefetch=2,
        grid=(1,),
        in_specs=[
            pl.BlockSpec((Z, 4, ROWS, HD), lambda i, step, half: (0, 0, 0, 0)),
            pl.BlockSpec((1, ROWS, 64), lambda i, step, half: (0, 0, 0)),
            pl.BlockSpec((1, 2, 20 * HD), lambda i, step, half: (step[0], 0, 0)),
            pl.BlockSpec((1, 2, 8 * HD), lambda i, step, half: (step[0], 0, 0)),
            pl.BlockSpec((20 * HD, 64), lambda i, step, half: (0, 0)),
            pl.BlockSpec((8 * HD, 64), lambda i, step, half: (0, 0)),
        ],
        out_specs=[pl.BlockSpec((1, ROWS, 64), lambda i, step, half: (0, 0, 0))] * 2,
    )
    velocity, advanced = pl.pallas_call(
        final_kernel,
        out_shape=(jax.ShapeDtypeStruct((1, ROWS, 64), f32),) * 2,
        grid_spec=grid_spec,
        compiler_params=params(16),
        name="final",
    )(step_index, half, got, latents, main_mod, guide_mod, main_head, guide_head)
    return velocity, advanced


def solution(mesh):
    fine = Mesh(mesh.devices.reshape(ZL, X, Y, ZH, CORE), ("zl", "x", "y", "zh", "core"))
    seq = ("x", "y", "zh", "core")
    return jax.shard_map(
        on_device,
        mesh=fine,
        in_specs=(P(seq, "zl", None),) * 3
        + (P(seq, None, "zl"),) * 3
        + (P(seq, "zl", None),)
        + (P(),) * 5,
        out_specs=(P(seq, "zl", None),) * 2,
        check_vma=False,
    )
```

```python
import math

import jax
import jax.numpy as jnp
from jax import lax
from jax.experimental import pallas as pl
from jax.experimental.pallas import tpu as pltpu
from jax.sharding import Mesh, PartitionSpec as P

HD = 128
STEPS = 50
ZL, X, Y, ZH, CORE = 4, 4, 4, 2, 2
Z = ZL * ZH
SIDE = 4
ROWS = 32
BLOCK = 128
COLUMN = ROWS * Z
TOKENS = COLUMN * CORE
TILE = 256
HEADS = 2
STAT = 32
KEYS = SIDE * TOKENS

guidance = 2.5
flow_shift = 3.0
epsilon = 1e-06
score_scale = math.log2(math.e) / math.sqrt(HD)

f32 = jnp.float32
bf16 = jnp.bfloat16
VMEM = pl.BlockSpec(memory_space=pltpu.VMEM)
SMEM = pl.BlockSpec(memory_space=pltpu.SMEM)
ANY = pl.BlockSpec(memory_space=pl.ANY)


def shape(*dims, dtype=bf16):
    return jax.ShapeDtypeStruct(dims, dtype)


def params(mib):
    return pltpu.CompilerParams(vmem_limit_bytes=mib * 1024 * 1024)


def pack_kernel(place, mq, mk, mv, gq, gk, gv, send, guide_send, guide_own, main, guide, sems):
    zh = place[0]
    copies = []
    for kind, ref in enumerate((mq, mk, mv)):
        copies.append(pltpu.make_async_copy(ref.at[0], main.at[kind], sems.at[kind]))
    for kind, ref in enumerate((gq, gk, gv)):
        copies.append(pltpu.make_async_copy(ref.at[0], guide.at[kind], sems.at[3 + kind]))
    for copy in copies:
        copy.start()
    for kind in range(3):
        copies[kind].wait()
        for zh_to in range(ZH):
            for zl_to in range(ZL):
                for slot in range(3):
                    head = zl_to * 5 + (4 if slot == 2 else 2 * zh_to + slot)
                    lanes = slice(head * HD, (head + 1) * HD)
                    send[zh_to * ZL + zl_to, slot * 3 + kind] = main[kind, :, lanes]
    own = pl.ds(pl.multiple_of(zh * HD, HD), HD)
    other = pl.ds(pl.multiple_of((1 - zh) * HD, HD), HD)
    for kind in range(3):
        copies[3 + kind].wait()
        guide_own[kind] = guide[kind, :, own]
        guide_send[kind] = guide[kind, :, other]


def unpack_kernel(
    place, got, sibling, guide_own, guide_core, guide_half, guide_across, queries, pairs
):
    zh, core = place[0], place[1]
    for ref, whose in ((got, core), (sibling, 1 - core)):
        base = whose * COLUMN
        for source in range(Z):
            rows = pl.ds(pl.multiple_of(base + source * ROWS, ROWS), ROWS)
            queries[rows, :] = ref[source, core * 3]
            for kind in range(2):
                pairs[kind, rows, :] = ref[source, core * 3 + 1 + kind]

    @pl.when(core == 0)
    def _():
        for ref, zh_from, core_from in (
            (guide_own, zh, 0),
            (guide_core, zh, 1),
            (guide_half, 1 - zh, 0),
            (guide_across, 1 - zh, 1),
        ):
            at = pl.multiple_of(core_from * COLUMN + zh_from * BLOCK, BLOCK)
            queries[pl.ds(pl.multiple_of(TOKENS + at, BLOCK), BLOCK), :] = ref[0]
            pairs[2, pl.ds(at, BLOCK), :] = ref[1]
            pairs[3, pl.ds(at, BLOCK), :] = ref[2]

    @pl.when(core == 1)
    def _():
        for ref, whose in ((got, 1), (sibling, 0)):
            for source in range(Z):
                rows = pl.ds(whose * COLUMN + source * ROWS, ROWS)
                for kind in range(2):
                    pairs[2 + kind, rows, :] = ref[source, 7 + kind]
            for zl in range(ZL):
                rows = pl.ds(TOKENS + whose * BLOCK + zl * ROWS, ROWS)
                queries[rows, :] = ref[zh * ZL + zl, 6]
        queries[pl.ds(TOKENS + COLUMN, COLUMN), :] = jnp.zeros((COLUMN, HD), bf16)


def diagonal():
    return lax.broadcasted_iota(jnp.int32, (HD, HD), 0) == lax.broadcasted_iota(
        jnp.int32, (HD, HD), 1
    )


def attend_kernel(queries, *refs):
    pairs, out = refs[:SIDE], refs[SIDE]
    values, scores, weights, stats = refs[SIDE + 1 :]
    for head in range(HEADS):
        for piece in range(SIDE):
            rows = pl.ds(piece * TOKENS, TOKENS)
            values[head, rows, :HD] = pairs[piece][head * 2 + 1]
            values[head, rows, HD:] = jnp.ones((TOKENS, HD), bf16)
    on_diagonal = diagonal()
    parts = [(piece, half) for piece in range(SIDE) for half in range(TOKENS // TILE)]
    tiles = HEADS * TOKENS // TILE

    def score_tile(tile):
        head = tile * TILE // TOKENS
        query = queries[tile * TILE : (tile + 1) * TILE, :]
        highest = None
        for index, (piece, half) in enumerate(parts):
            part = lax.dot_general(
                query,
                pairs[piece][head * 2, half * TILE : (half + 1) * TILE, :],
                (((1,), (1,)), ((), ())),
                preferred_element_type=f32,
            )
            scores[tile, :, index * TILE : (index + 1) * TILE] = part
            here = jnp.maximum(part[:, :HD], part[:, HD:])
            highest = here if highest is None else jnp.maximum(highest, here)
        return jnp.max(highest, axis=1, keepdims=True) * score_scale

    def weight_tile(tile, highest):
        for index in range(len(parts)):
            columns = slice(index * TILE, (index + 1) * TILE)
            part = scores[tile, :, columns]
            weights[tile, :, columns] = jnp.exp2(part * score_scale - highest).astype(bf16)
        total = jnp.dot(
            weights[tile], values[tile * TILE // TOKENS], preferred_element_type=f32
        )
        weight_sum = total[:, HD:]
        out[tile * TILE : (tile + 1) * TILE, :] = (total[:, :HD] / weight_sum).astype(bf16)
        level = highest + jnp.log2(weight_sum)
        for part in range(TILE // HD):
            block = level[part * HD : (part + 1) * HD, :]
            row = jnp.sum(jnp.where(on_diagonal, block, 0.0), axis=0, keepdims=True)
            stats[tile * (TILE // HD) + part : tile * (TILE // HD) + part + 1, :] = row

    tops = [score_tile(0)]
    for tile in range(tiles):
        if tile + 1 < tiles:
            tops.append(score_tile(tile + 1))
        weight_tile(tile, tops[tile])
    level = stats[...]
    high = level.astype(bf16).astype(f32)
    middle = (level - high).astype(bf16).astype(f32)
    low = level - high - middle
    block = jnp.concatenate([high, middle, low, jnp.zeros_like(low)], axis=0)
    out[HEADS * TOKENS :, :] = block.astype(bf16)


def combine_kernel(place, *refs):
    parts, send = refs[:SIDE], refs[SIDE]
    on_diagonal = diagonal()
    levels = []
    for part in parts:
        block = part[HEADS * TOKENS :, :].astype(f32)
        levels.append(block[0:8] + block[8:16] + block[16:24])
    top = levels[0]
    for level in levels[1:]:
        top = jnp.maximum(top, level)
    shares = [jnp.exp2(level - top) for level in levels]
    whole = shares[0] + shares[1] + shares[2] + shares[3]
    shares = [share / whole for share in shares]
    results = []
    for tile in range(HEADS * TOKENS // HD):
        total = None
        for part, share in zip(parts, shares):
            row = jnp.broadcast_to(share[tile : tile + 1, :], (HD, HD))
            column = jnp.sum(jnp.where(on_diagonal, row, 0.0), axis=1, keepdims=True)
            term = part[tile * HD : (tile + 1) * HD, :].astype(f32) * column
            total = term if total is None else total + term
        results.append(total.astype(bf16))

    def put(head, tiles):
        for tile, result in enumerate(tiles):
            for zl in range(ZL):
                send[tile * ZL + zl, head] = result[zl * ROWS : (zl + 1) * ROWS, :]

    blocks = TOKENS // HD
    put(0, results[:blocks])

    @pl.when(place[1] == 0)
    def _():
        put(1, results[blocks:])

    @pl.when(place[1] == 1)
    def _():
        put(1, [results[blocks + tile // ZH] for tile in range(blocks)])


def split_dot(left, weight):
    high = left.astype(bf16)
    low = (left - high.astype(f32)).astype(bf16)
    return jnp.dot(high, weight, preferred_element_type=f32) + jnp.dot(
        low, weight, preferred_element_type=f32
    )


def flow_of(heads, table, weight):
    width = len(heads) * HD
    center = sum(jnp.sum(h, axis=1, keepdims=True) for h in heads) / width
    centered = [h - center for h in heads]
    spread = sum(jnp.sum(h * h, axis=1, keepdims=True) for h in centered) / width
    shrink = lax.rsqrt(spread + epsilon)
    shift, scale = table[0, 0:1, :].astype(f32), table[0, 1:2, :].astype(f32)
    total = None
    for index, head in enumerate(centered):
        lanes = slice(index * HD, (index + 1) * HD)
        modulated = head * shrink * (1.0 + scale[:, lanes]) + shift[:, lanes]
        term = split_dot(modulated, weight[lanes, :])
        total = term if total is None else total + term
    return total


def sigma_at(index):
    remaining = 1.0 - index.astype(f32) / STEPS
    return flow_shift * remaining / (1.0 + (flow_shift - 1.0) * remaining)


def final_kernel(
    step,
    place,
    got,
    latents,
    main_mod,
    guide_mod,
    main_head,
    guide_head,
    velocity,
    advanced,
):
    zh = place[0]
    main, guide = [], []
    for zl in range(ZL):
        for zh_from in range(ZH):
            main += [got[core * Z + zh_from * ZL + zl, 0] for core in range(CORE)]
            guide += [got[zh_from * ZL + zl, 1]]
        main += [got[Z + zh * ZL + zl, 1]]
    main_flow = flow_of([h.astype(f32) for h in main], main_mod, main_head)
    guide_flow = flow_of([h.astype(f32) for h in guide], guide_mod, guide_head)
    result = guide_flow + guidance * (main_flow - guide_flow)
    now = jnp.full((1, 1), step[0], jnp.int32)
    velocity[0] = result
    advanced[0] = latents[0] + (sigma_at(now + 1) - sigma_at(now)) * result


def plane_shift(array, by, axis_of_core):
    pairs = []
    for x in range(X):
        for y in range(Y):
            for core in range(CORE):
                if axis_of_core[core] == "x":
                    to = ((x + by) % X, y)
                else:
                    to = (x, (y + by) % Y)
                pairs.append(((x * Y + y) * CORE + core, (to[0] * Y + to[1]) * CORE + core))
    return lax.ppermute(array, ("x", "y", "core"), pairs)


SHIFTS = (2, 1, -1)


def attend(queries, pairs):
    return pl.pallas_call(
        attend_kernel,
        out_shape=shape(HEADS * TOKENS + STAT, HD),
        in_specs=[VMEM] * (1 + SIDE),
        out_specs=VMEM,
        scratch_shapes=[
            pltpu.VMEM((HEADS, KEYS, 2 * HD), bf16),
            pltpu.VMEM((HEADS * TOKENS // TILE, TILE, KEYS), f32),
            pltpu.VMEM((HEADS * TOKENS // TILE, TILE, KEYS), bf16),
            pltpu.VMEM((8, HD), f32),
        ],
        compiler_params=params(32),
        cost_estimate=pl.CostEstimate(
            flops=4 * HEADS * TOKENS * KEYS * HD,
            bytes_accessed=4 * HEADS * KEYS * HD,
            transcendentals=HEADS * TOKENS * KEYS,
        ),
        name="attend",
    )(queries, *pairs)


def on_device(
    main_query,
    main_key,
    main_value,
    guide_query,
    guide_key,
    guide_value,
    latents,
    step_index,
    main_mod,
    guide_mod,
    main_head,
    guide_head,
):
    zh, core = lax.axis_index("zh"), lax.axis_index("core")
    place = jnp.stack([zh, core]).astype(jnp.int32)
    send, guide_send, guide_own = pl.pallas_call(
        pack_kernel,
        out_shape=(shape(Z, 9, ROWS, HD), shape(3, BLOCK, HD), shape(3, BLOCK, HD)),
        in_specs=[SMEM] + [ANY] * 6,
        out_specs=(VMEM,) * 3,
        scratch_shapes=[
            pltpu.VMEM((3, ROWS, 20 * HD), bf16),
            pltpu.VMEM((3, BLOCK, 2 * HD), bf16),
            pltpu.SemaphoreType.DMA((6,)),
        ],
        compiler_params=params(60),
        name="pack",
    )(place, main_query, main_key, main_value, guide_query, guide_key, guide_value)
    halves = ("zh", "core")
    guide_core = lax.ppermute(guide_own, halves, [(1, 0), (3, 2)])
    guide_half = lax.ppermute(guide_send, halves, [(0, 2), (2, 0)])
    guide_across = lax.ppermute(guide_send, halves, [(1, 2), (3, 0)])
    got = lax.all_to_all(send, ("zh", "zl"), split_axis=0, concat_axis=0, tiled=True)
    got, guide_core, guide_half, guide_across = lax.optimization_barrier(
        (got, guide_core, guide_half, guide_across)
    )
    sibling = lax.ppermute(got, "core", [(0, 1), (1, 0)])
    queries, pairs = pl.pallas_call(
        unpack_kernel,
        out_shape=(shape(HEADS * TOKENS, HD), shape(2 * HEADS, TOKENS, HD)),
        in_specs=[SMEM] + [VMEM] * 6,
        out_specs=(VMEM,) * 2,
        compiler_params=params(16),
        name="unpack",
    )(place, got, sibling, guide_own, guide_core, guide_half, guide_across)
    all_pairs = [pairs] + [plane_shift(pairs, by, "yx") for by in SHIFTS]
    parts = [attend(queries, all_pairs)]
    for by in SHIFTS:
        arrived, parts[0] = lax.optimization_barrier((plane_shift(queries, by, "xy"), parts[0]))
        part = attend(arrived, all_pairs)
        parts.append(plane_shift(part, -by, "xy"))
    send = pl.pallas_call(
        combine_kernel,
        out_shape=shape(CORE * Z, HEADS, ROWS, HD),
        in_specs=[SMEM] + [VMEM] * SIDE,
        out_specs=VMEM,
        compiler_params=params(16),
        name="combine",
    )(place, *parts)
    got = lax.all_to_all(send, ("core", "zh", "zl"), split_axis=0, concat_axis=0, tiled=True)

    whole = lambda *dims: pl.BlockSpec(dims, lambda i, step, place: (0,) * len(dims))
    row = lambda *dims: pl.BlockSpec(dims, lambda i, step, place: (step[0], 0, 0))
    velocity, advanced = pl.pallas_call(
        final_kernel,
        out_shape=(shape(1, ROWS, 64, dtype=f32),) * 2,
        grid_spec=pltpu.PrefetchScalarGridSpec(
            num_scalar_prefetch=2,
            grid=(1,),
            in_specs=[
                whole(CORE * Z, HEADS, ROWS, HD),
                whole(1, ROWS, 64),
                row(1, 2, 20 * HD),
                row(1, 2, 8 * HD),
                whole(20 * HD, 64),
                whole(8 * HD, 64),
            ],
            out_specs=[whole(1, ROWS, 64)] * 2,
        ),
        compiler_params=params(16),
        name="final",
    )(step_index, place, got, latents, main_mod, guide_mod, main_head, guide_head)
    return velocity, advanced


def solution(mesh):
    fine = Mesh(mesh.devices.reshape(ZL, X, Y, ZH, CORE), ("zl", "x", "y", "zh", "core"))
    seq = ("x", "y", "zh", "core")
    return jax.shard_map(
        on_device,
        mesh=fine,
        in_specs=(P(seq, "zl", None),) * 3
        + (P(seq, None, "zl"),) * 3
        + (P(seq, "zl", None),)
        + (P(),) * 5,
        out_specs=(P(seq, "zl", None),) * 2,
        check_vma=False,
    )
```

```python
import math

import jax
import jax.numpy as jnp
from jax import lax
from jax.experimental import pallas as pl
from jax.experimental.pallas import tpu as pltpu
from jax.sharding import Mesh, PartitionSpec as P

HD = 128
STEPS = 50
ZL, X, Y, ZH, CORE = 4, 4, 4, 2, 2
Z = ZL * ZH
SIDE = 4
ROWS = 32
BLOCK = 128
COLUMN = ROWS * Z
TOKENS = COLUMN * CORE
TILE = 256
HEADS = 2
STAT = 32
KEYS = SIDE * TOKENS

guidance = 2.5
flow_shift = 3.0
epsilon = 1e-06
score_scale = math.log2(math.e) / math.sqrt(HD)

f32 = jnp.float32
bf16 = jnp.bfloat16
VMEM = pl.BlockSpec(memory_space=pltpu.VMEM)
SMEM = pl.BlockSpec(memory_space=pltpu.SMEM)
ANY = pl.BlockSpec(memory_space=pl.ANY)


def shape(*dims, dtype=bf16):
    return jax.ShapeDtypeStruct(dims, dtype)


def params(mib):
    return pltpu.CompilerParams(vmem_limit_bytes=mib * 1024 * 1024)


def pack_kernel(place, mq, mk, mv, gq, gk, gv, send, guide_send, guide_own, main, guide, sems):
    zh = place[0]
    copies = []
    for kind, ref in enumerate((mq, mk, mv)):
        copies.append(pltpu.make_async_copy(ref.at[0], main.at[kind], sems.at[kind]))
    for kind, ref in enumerate((gq, gk, gv)):
        copies.append(pltpu.make_async_copy(ref.at[0], guide.at[kind], sems.at[3 + kind]))
    for copy in copies:
        copy.start()
    for kind in range(3):
        copies[kind].wait()
        for zh_to in range(ZH):
            for zl_to in range(ZL):
                for slot in range(3):
                    head = zl_to * 5 + (4 if slot == 2 else 2 * zh_to + slot)
                    lanes = slice(head * HD, (head + 1) * HD)
                    send[zh_to * ZL + zl_to, slot * 3 + kind] = main[kind, :, lanes]
    own = pl.ds(pl.multiple_of(zh * HD, HD), HD)
    other = pl.ds(pl.multiple_of((1 - zh) * HD, HD), HD)
    for kind in range(3):
        copies[3 + kind].wait()
        guide_own[kind] = guide[kind, :, own]
        guide_send[kind] = guide[kind, :, other]


def unpack_kernel(
    place, got, sibling, guide_own, guide_core, guide_half, guide_across, queries, pairs
):
    zh, core = place[0], place[1]
    for ref, whose in ((got, core), (sibling, 1 - core)):
        base = whose * COLUMN
        for source in range(Z):
            rows = pl.ds(pl.multiple_of(base + source * ROWS, ROWS), ROWS)
            queries[rows, :] = ref[source, core * 3]
            for kind in range(2):
                pairs[kind, rows, :] = ref[source, core * 3 + 1 + kind]

    @pl.when(core == 0)
    def _():
        for ref, zh_from, core_from in (
            (guide_own, zh, 0),
            (guide_core, zh, 1),
            (guide_half, 1 - zh, 0),
            (guide_across, 1 - zh, 1),
        ):
            at = pl.multiple_of(core_from * COLUMN + zh_from * BLOCK, BLOCK)
            queries[pl.ds(pl.multiple_of(TOKENS + at, BLOCK), BLOCK), :] = ref[0]
            pairs[2, pl.ds(at, BLOCK), :] = ref[1]
            pairs[3, pl.ds(at, BLOCK), :] = ref[2]

    @pl.when(core == 1)
    def _():
        for ref, whose in ((got, 1), (sibling, 0)):
            for source in range(Z):
                rows = pl.ds(whose * COLUMN + source * ROWS, ROWS)
                for kind in range(2):
                    pairs[2 + kind, rows, :] = ref[source, 7 + kind]
            for zl in range(ZL):
                rows = pl.ds(TOKENS + whose * BLOCK + zl * ROWS, ROWS)
                queries[rows, :] = ref[zh * ZL + zl, 6]
        queries[pl.ds(TOKENS + COLUMN, COLUMN), :] = jnp.zeros((COLUMN, HD), bf16)


def diagonal():
    return lax.broadcasted_iota(jnp.int32, (HD, HD), 0) == lax.broadcasted_iota(
        jnp.int32, (HD, HD), 1
    )


def attend_kernel(queries, *refs):
    pairs, out = refs[:SIDE], refs[SIDE]
    values, scores, weights, stats = refs[SIDE + 1 :]
    for head in range(HEADS):
        for piece in range(SIDE):
            rows = pl.ds(piece * TOKENS, TOKENS)
            values[head, rows, :HD] = pairs[piece][head * 2 + 1]
            values[head, rows, HD:] = jnp.ones((TOKENS, HD), bf16)
    on_diagonal = diagonal()
    parts = [(piece, half) for piece in range(SIDE) for half in range(TOKENS // TILE)]
    tiles = range(HEADS * TOKENS // TILE)
    tops = []
    for tile in tiles:
        head = tile * TILE // TOKENS
        query = queries[tile * TILE : (tile + 1) * TILE, :]
        highest = None
        for index, (piece, half) in enumerate(parts):
            part = lax.dot_general(
                query,
                pairs[piece][head * 2, half * TILE : (half + 1) * TILE, :],
                (((1,), (1,)), ((), ())),
                preferred_element_type=f32,
            )
            scores[tile, :, index * TILE : (index + 1) * TILE] = part
            here = jnp.maximum(part[:, :HD], part[:, HD:])
            highest = here if highest is None else jnp.maximum(highest, here)
        tops.append(jnp.max(highest, axis=1, keepdims=True) * score_scale)
    for tile in tiles:
        for index in range(len(parts)):
            columns = slice(index * TILE, (index + 1) * TILE)
            part = scores[tile, :, columns]
            weights[tile, :, columns] = jnp.exp2(part * score_scale - tops[tile]).astype(bf16)
    for tile in tiles:
        total = jnp.dot(
            weights[tile], values[tile * TILE // TOKENS], preferred_element_type=f32
        )
        weight_sum = total[:, HD:]
        out[tile * TILE : (tile + 1) * TILE, :] = (total[:, :HD] / weight_sum).astype(bf16)
        level = tops[tile] + jnp.log2(weight_sum)
        for part in range(TILE // HD):
            block = level[part * HD : (part + 1) * HD, :]
            row = jnp.sum(jnp.where(on_diagonal, block, 0.0), axis=0, keepdims=True)
            stats[tile * (TILE // HD) + part : tile * (TILE // HD) + part + 1, :] = row
    level = stats[...]
    high = level.astype(bf16).astype(f32)
    middle = (level - high).astype(bf16).astype(f32)
    low = level - high - middle
    block = jnp.concatenate([high, middle, low, jnp.zeros_like(low)], axis=0)
    out[HEADS * TOKENS :, :] = block.astype(bf16)


def combine_kernel(place, *refs):
    parts, send = refs[:SIDE], refs[SIDE]
    levels = []
    for part in parts:
        block = part[HEADS * TOKENS :, :].astype(f32)
        levels.append(block[0:8] + block[8:16] + block[16:24])
    top = levels[0]
    for level in levels[1:]:
        top = jnp.maximum(top, level)
    shares = [jnp.exp2(level - top) for level in levels]
    whole = shares[0] + shares[1] + shares[2] + shares[3]
    filler = jnp.zeros((HD - 8, HD), f32)
    shares = [jnp.transpose(jnp.concatenate([share / whole, filler], axis=0)) for share in shares]
    results = []
    for tile in range(HEADS * TOKENS // HD):
        total = None
        for part, share in zip(parts, shares):
            column = share[:, tile : tile + 1]
            term = part[tile * HD : (tile + 1) * HD, :].astype(f32) * column
            total = term if total is None else total + term
        results.append(total.astype(bf16))

    def put(head, tiles):
        for tile, result in enumerate(tiles):
            for zl in range(ZL):
                send[tile * ZL + zl, head] = result[zl * ROWS : (zl + 1) * ROWS, :]

    blocks = TOKENS // HD
    put(0, results[:blocks])

    @pl.when(place[1] == 0)
    def _():
        put(1, results[blocks:])

    @pl.when(place[1] == 1)
    def _():
        put(1, [results[blocks + tile // ZH] for tile in range(blocks)])


def flow_of(heads, table, weight):
    width = len(heads) * HD
    center = jnp.sum(sum(heads), axis=1, keepdims=True) / width
    centered = [h - center for h in heads]
    spread = jnp.sum(sum(h * h for h in centered), axis=1, keepdims=True) / width
    shrink = lax.rsqrt(spread + epsilon)
    shift, scale = table[0, 0:1, :].astype(f32), table[0, 1:2, :].astype(f32)
    modulated = jnp.concatenate(centered, axis=1) * shrink * (1.0 + scale) + shift
    high = modulated.astype(bf16)
    low = (modulated - high.astype(f32)).astype(bf16)
    both = jnp.dot(
        jnp.concatenate([high, low], axis=0), weight[...], preferred_element_type=f32
    )
    return both[:ROWS] + both[ROWS:]


def sigma_at(index):
    remaining = 1.0 - index.astype(f32) / STEPS
    return flow_shift * remaining / (1.0 + (flow_shift - 1.0) * remaining)


def final_kernel(
    step,
    place,
    got,
    latents,
    main_mod,
    guide_mod,
    main_head,
    guide_head,
    velocity,
    advanced,
):
    zh = place[0]
    main, guide = [], []
    for zl in range(ZL):
        for zh_from in range(ZH):
            main += [got[core * Z + zh_from * ZL + zl, 0] for core in range(CORE)]
            guide += [got[zh_from * ZL + zl, 1]]
        main += [got[Z + zh * ZL + zl, 1]]
    main_flow = flow_of([h.astype(f32) for h in main], main_mod, main_head)
    guide_flow = flow_of([h.astype(f32) for h in guide], guide_mod, guide_head)
    result = guide_flow + guidance * (main_flow - guide_flow)
    now = jnp.full((1, 1), step[0], jnp.int32)
    velocity[0] = result
    advanced[0] = latents[0] + (sigma_at(now + 1) - sigma_at(now)) * result


def plane_shift(array, by, axis_of_core):
    pairs = []
    for x in range(X):
        for y in range(Y):
            for core in range(CORE):
                if axis_of_core[core] == "x":
                    to = ((x + by) % X, y)
                else:
                    to = (x, (y + by) % Y)
                pairs.append(((x * Y + y) * CORE + core, (to[0] * Y + to[1]) * CORE + core))
    return lax.ppermute(array, ("x", "y", "core"), pairs)


SHIFTS = (2, 1, -1)


def attend(queries, pairs):
    rows, tiles = HEADS * TOKENS, HEADS * TOKENS // TILE
    return pl.pallas_call(
        attend_kernel,
        out_shape=shape(rows + STAT, HD),
        in_specs=[VMEM] * (1 + SIDE),
        out_specs=VMEM,
        scratch_shapes=[
            pltpu.VMEM((HEADS, KEYS, 2 * HD), bf16),
            pltpu.VMEM((tiles, TILE, KEYS), f32),
            pltpu.VMEM((tiles, TILE, KEYS), bf16),
            pltpu.VMEM((8, HD), f32),
        ],
        compiler_params=params(32),
        cost_estimate=pl.CostEstimate(
            flops=4 * rows * KEYS * HD,
            bytes_accessed=4 * HEADS * KEYS * HD,
            transcendentals=rows * KEYS,
        ),
        name="attend",
    )(queries, *pairs)


def on_device(
    main_query,
    main_key,
    main_value,
    guide_query,
    guide_key,
    guide_value,
    latents,
    step_index,
    main_mod,
    guide_mod,
    main_head,
    guide_head,
):
    zh, core = lax.axis_index("zh"), lax.axis_index("core")
    place = jnp.stack([zh, core]).astype(jnp.int32)
    send, guide_send, guide_own = pl.pallas_call(
        pack_kernel,
        out_shape=(shape(Z, 9, ROWS, HD), shape(3, BLOCK, HD), shape(3, BLOCK, HD)),
        in_specs=[SMEM] + [ANY] * 6,
        out_specs=(VMEM,) * 3,
        scratch_shapes=[
            pltpu.VMEM((3, ROWS, 20 * HD), bf16),
            pltpu.VMEM((3, BLOCK, 2 * HD), bf16),
            pltpu.SemaphoreType.DMA((6,)),
        ],
        compiler_params=params(60),
        name="pack",
    )(place, main_query, main_key, main_value, guide_query, guide_key, guide_value)
    halves = ("zh", "core")
    guide_core = lax.ppermute(guide_own, halves, [(1, 0), (3, 2)])
    guide_half = lax.ppermute(guide_send, halves, [(0, 2), (2, 0)])
    guide_across = lax.ppermute(guide_send, halves, [(1, 2), (3, 0)])
    got = lax.all_to_all(send, ("zh", "zl"), split_axis=0, concat_axis=0, tiled=True)
    got, guide_core, guide_half, guide_across = lax.optimization_barrier(
        (got, guide_core, guide_half, guide_across)
    )
    sibling = lax.ppermute(got, "core", [(0, 1), (1, 0)])
    queries, pairs = pl.pallas_call(
        unpack_kernel,
        out_shape=(shape(HEADS * TOKENS, HD), shape(2 * HEADS, TOKENS, HD)),
        in_specs=[SMEM] + [VMEM] * 6,
        out_specs=(VMEM,) * 2,
        compiler_params=params(16),
        name="unpack",
    )(place, got, sibling, guide_own, guide_core, guide_half, guide_across)
    all_queries = [queries] + [plane_shift(queries, by, "xy") for by in SHIFTS]
    all_pairs = [pairs] + [plane_shift(pairs, by, "yx") for by in SHIFTS]
    parts = [attend(q, all_pairs) for q in all_queries]
    parts[1:] = [plane_shift(p, -by, "xy") for p, by in zip(parts[1:], SHIFTS)]
    send = pl.pallas_call(
        combine_kernel,
        out_shape=shape(CORE * Z, HEADS, ROWS, HD),
        in_specs=[SMEM] + [VMEM] * SIDE,
        out_specs=VMEM,
        compiler_params=params(16),
        name="combine",
    )(place, *parts)
    got = lax.all_to_all(send, ("core", "zh", "zl"), split_axis=0, concat_axis=0, tiled=True)

    whole = lambda *dims: pl.BlockSpec(dims, lambda i, step, place: (0,) * len(dims))
    row = lambda *dims: pl.BlockSpec(dims, lambda i, step, place: (step[0], 0, 0))
    velocity, advanced = pl.pallas_call(
        final_kernel,
        out_shape=(shape(1, ROWS, 64, dtype=f32),) * 2,
        grid_spec=pltpu.PrefetchScalarGridSpec(
            num_scalar_prefetch=2,
            grid=(1,),
            in_specs=[
                whole(CORE * Z, HEADS, ROWS, HD),
                whole(1, ROWS, 64),
                row(1, 2, 20 * HD),
                row(1, 2, 8 * HD),
                whole(20 * HD, 64),
                whole(8 * HD, 64),
            ],
            out_specs=[whole(1, ROWS, 64)] * 2,
        ),
        compiler_params=params(16),
        name="final",
    )(step_index, place, got, latents, main_mod, guide_mod, main_head, guide_head)
    return velocity, advanced


def solution(mesh):
    fine = Mesh(mesh.devices.reshape(ZL, X, Y, ZH, CORE), ("zl", "x", "y", "zh", "core"))
    seq = ("x", "y", "zh", "core")
    return jax.shard_map(
        on_device,
        mesh=fine,
        in_specs=(P(seq, "zl", None),) * 3
        + (P(seq, None, "zl"),) * 3
        + (P(seq, "zl", None),)
        + (P(),) * 5,
        out_specs=(P(seq, "zl", None),) * 2,
        check_vma=False,
    )
```

```python
import math

import jax
import jax.numpy as jnp
from jax import lax
from jax.experimental import pallas as pl
from jax.experimental.pallas import tpu as pltpu
from jax.sharding import Mesh, PartitionSpec as P

HD = 128
C = 64
STEPS = 50
ZL, X, Y, ZH, CORE = 4, 4, 4, 2, 2
Z = ZL * ZH
SIDE = 4
ROWS = 32
BLOCK = 128
COLUMN = ROWS * Z
TOKENS = COLUMN * CORE
TILE = 256
HEADS = 2
STAT = 32
KEYS = SIDE * TOKENS

guidance = 2.5
flow_shift = 3.0
epsilon = 1e-06
score_scale = math.log2(math.e) / math.sqrt(HD)

f32 = jnp.float32
bf16 = jnp.bfloat16
VMEM = pl.BlockSpec(memory_space=pltpu.VMEM)
SMEM = pl.BlockSpec(memory_space=pltpu.SMEM)
ANY = pl.BlockSpec(memory_space=pl.ANY)


def shape(*dims, dtype=bf16):
    return jax.ShapeDtypeStruct(dims, dtype)


def params(mib):
    return pltpu.CompilerParams(vmem_limit_bytes=mib * 1024 * 1024)


def pack_guide_kernel(place, gq, gk, gv, send, own, sems):
    copies = []
    for head, to in ((1 - place[0], send), (place[0], own)):
        lanes = pl.ds(pl.multiple_of(head * HD, HD), HD)
        for kind, ref in enumerate((gq, gk, gv)):
            copy = pltpu.make_async_copy(ref.at[0, :, lanes], to.at[kind], sems.at[len(copies)])
            copy.start()
            copies.append(copy)
    for copy in copies:
        copy.wait()


def pack_kernel(mq, mk, mv, send, main, sems):
    copies = []
    for kind, ref in enumerate((mq, mk, mv)):
        copy = pltpu.make_async_copy(ref.at[0], main.at[kind], sems.at[kind])
        copy.start()
        copies.append(copy)
    for kind, copy in enumerate(copies):
        copy.wait()
        for zh_to in range(ZH):
            for zl_to in range(ZL):
                for slot in range(3):
                    head = zl_to * 5 + (4 if slot == 2 else 2 * zh_to + slot)
                    lanes = slice(head * HD, (head + 1) * HD)
                    send[zh_to * ZL + zl_to, slot * 3 + kind] = main[kind, :, lanes]


def unpack_kernel(
    place, got, sibling, guide_own, guide_core, guide_half, guide_across, queries, pairs
):
    zh, core = place[0], place[1]
    for ref, whose in ((got, core), (sibling, 1 - core)):
        base = whose * COLUMN
        for source in range(Z):
            rows = pl.ds(pl.multiple_of(base + source * ROWS, ROWS), ROWS)
            queries[rows, :] = ref[source, core * 3]
            for kind in range(2):
                pairs[kind, rows, :] = ref[source, core * 3 + 1 + kind]

    @pl.when(core == 0)
    def _():
        for ref, zh_from, core_from in (
            (guide_own, zh, 0),
            (guide_core, zh, 1),
            (guide_half, 1 - zh, 0),
            (guide_across, 1 - zh, 1),
        ):
            at = pl.multiple_of(core_from * COLUMN + zh_from * BLOCK, BLOCK)
            queries[pl.ds(pl.multiple_of(TOKENS + at, BLOCK), BLOCK), :] = ref[0]
            pairs[2, pl.ds(at, BLOCK), :] = ref[1]
            pairs[3, pl.ds(at, BLOCK), :] = ref[2]

    @pl.when(core == 1)
    def _():
        for ref, whose in ((got, 1), (sibling, 0)):
            for source in range(Z):
                rows = pl.ds(whose * COLUMN + source * ROWS, ROWS)
                for kind in range(2):
                    pairs[2 + kind, rows, :] = ref[source, 7 + kind]
            for zl in range(ZL):
                rows = pl.ds(TOKENS + whose * BLOCK + zl * ROWS, ROWS)
                queries[rows, :] = ref[zh * ZL + zl, 6]
        queries[pl.ds(TOKENS + COLUMN, COLUMN), :] = jnp.zeros((COLUMN, HD), bf16)


def diagonal():
    return lax.broadcasted_iota(jnp.int32, (HD, HD), 0) == lax.broadcasted_iota(
        jnp.int32, (HD, HD), 1
    )


def attend_kernel(queries, *refs):
    pairs, out = refs[:SIDE], refs[SIDE]
    values, scores, weights, stats = refs[SIDE + 1 :]
    for head in range(HEADS):
        for piece in range(SIDE):
            rows = pl.ds(piece * TOKENS, TOKENS)
            values[head, rows, :HD] = pairs[piece][head * 2 + 1]
            values[head, rows, HD:] = jnp.ones((TOKENS, HD), bf16)
    on_diagonal = diagonal()
    parts = [(piece, half) for piece in range(SIDE) for half in range(TOKENS // TILE)]
    tiles = range(HEADS * TOKENS // TILE)
    tops = []
    for tile in tiles:
        head = tile * TILE // TOKENS
        query = queries[tile * TILE : (tile + 1) * TILE, :]
        highest = None
        for index, (piece, half) in enumerate(parts):
            part = lax.dot_general(
                query,
                pairs[piece][head * 2, half * TILE : (half + 1) * TILE, :],
                (((1,), (1,)), ((), ())),
                preferred_element_type=f32,
            )
            scores[tile, :, index * TILE : (index + 1) * TILE] = part
            here = jnp.maximum(part[:, :HD], part[:, HD:])
            highest = here if highest is None else jnp.maximum(highest, here)
        tops.append(jnp.max(highest, axis=1, keepdims=True) * score_scale)
    for tile in tiles:
        for index in range(len(parts)):
            columns = slice(index * TILE, (index + 1) * TILE)
            part = scores[tile, :, columns]
            weights[tile, :, columns] = jnp.exp2(part * score_scale - tops[tile]).astype(bf16)
    for tile in tiles:
        total = jnp.dot(
            weights[tile], values[tile * TILE // TOKENS], preferred_element_type=f32
        )
        weight_sum = total[:, HD:]
        out[tile * TILE : (tile + 1) * TILE, :] = (total[:, :HD] / weight_sum).astype(bf16)
        level = tops[tile] + jnp.log2(weight_sum)
        for part in range(TILE // HD):
            block = level[part * HD : (part + 1) * HD, :]
            row = jnp.sum(jnp.where(on_diagonal, block, 0.0), axis=0, keepdims=True)
            stats[tile * (TILE // HD) + part : tile * (TILE // HD) + part + 1, :] = row
    level = stats[...]
    high = level.astype(bf16).astype(f32)
    middle = (level - high).astype(bf16).astype(f32)
    low = level - high - middle
    block = jnp.concatenate([high, middle, low, jnp.zeros_like(low)], axis=0)
    out[HEADS * TOKENS :, :] = block.astype(bf16)


def terms(value):
    high = value.astype(bf16)
    low = (value - high.astype(f32)).astype(bf16)
    return jnp.concatenate([high, low], axis=0)


def term_dot(value, weight):
    both = jnp.dot(terms(value), weight, preferred_element_type=f32)
    return both[: value.shape[0]] + both[value.shape[0] :]


def prepare_kernel(
    step, place, main_mod, guide_mod, main_head, guide_head, weights, scales, means, shifts
):
    zh, core, zl = place[0], place[1], place[2]
    first = pl.ds(pl.multiple_of((zl * 5 + 2 * zh + core) * HD, HD), HD)
    shared = pl.ds(pl.multiple_of((zl * 5 + 4) * HD, HD), HD)
    guide = pl.ds(pl.multiple_of((zl * 2 + zh) * HD, HD), HD)
    weights[0] = main_head[first, :]
    scales[...] = jnp.zeros_like(scales)
    scales[0:1, :] = 1.0 + main_mod[0, :, first][1:2].astype(f32)

    @pl.when(core == 0)
    def _():
        weights[1] = guide_head[guide, :]
        scales[1:2, :] = 1.0 + guide_mod[0, :, guide][1:2].astype(f32)

    @pl.when(core == 1)
    def _():
        weights[1] = main_head[shared, :]
        scales[1:2, :] = 1.0 + main_mod[0, :, shared][1:2].astype(f32)

    def rows_of(table, order):
        shift, scale = table[0, 0:1, :].astype(f32), 1.0 + table[0, 1:2, :].astype(f32)
        owner = lax.broadcasted_iota(jnp.int32, scale.shape, 1) >> 7
        rows = [jnp.where(owner == head, scale, 0.0) for head in order] + [shift]
        rows += [jnp.zeros_like(shift)] * (-len(rows) % 8)
        return jnp.concatenate(rows, axis=0)

    main_order = [
        zl * 5 + 2 * zh + core for core in range(CORE) for zh in range(ZH) for zl in range(ZL)
    ] + [zl * 5 + 4 for zl in range(ZL)]
    guide_order = [zl * 2 + zh for zh in range(ZH) for zl in range(ZL)]
    main_rows = term_dot(rows_of(main_mod, main_order), main_head[...])
    guide_rows = term_dot(rows_of(guide_mod, guide_order), guide_head[...])
    main_rows = jnp.concatenate([main_rows, jnp.zeros_like(main_rows)], axis=1)
    guide_rows = jnp.concatenate([jnp.zeros_like(guide_rows), guide_rows], axis=1)
    means[...] = jnp.zeros_like(means)
    for source in range(CORE * Z):
        means[source * 8 : source * 8 + 1, :] = main_rows[source : source + 1]
    for source in range(Z):
        means[source * 8 + 4 : source * 8 + 5, :] = guide_rows[source : source + 1]
        at = (Z + source) * 8 + 4
        means[at : at + 1, :] = main_rows[2 * Z + source % ZL : 2 * Z + source % ZL + 1]
    shifts[...] = jnp.zeros_like(shifts)
    shifts[0:1, :] = main_rows[20:21] + guide_rows[8:9]


def combine_kernel(place, weights, scales, *refs):
    parts, send = refs[:SIDE], refs[SIDE]
    on_diagonal = diagonal()
    levels = []
    for part in parts:
        block = part[HEADS * TOKENS :, :].astype(f32)
        levels.append(block[0:8] + block[8:16] + block[16:24])
    top = levels[0]
    for level in levels[1:]:
        top = jnp.maximum(top, level)
    shares = [jnp.exp2(level - top) for level in levels]
    whole = shares[0] + shares[1] + shares[2] + shares[3]
    filler = jnp.zeros((HD - 8, HD), f32)
    shares = [jnp.transpose(jnp.concatenate([share / whole, filler], axis=0)) for share in shares]
    blocks = TOKENS // HD
    flows, stats = [], []
    for head in range(HEADS):
        merged = []
        for tile in range(head * blocks, (head + 1) * blocks):
            total = None
            for part, share in zip(parts, shares):
                column = share[:, tile : tile + 1]
                term = part[tile * HD : (tile + 1) * HD, :].astype(f32) * column
                total = term if total is None else total + term
            merged.append(total)
        attended = jnp.concatenate(merged, axis=0).astype(bf16).astype(f32)
        mean = jnp.mean(attended, axis=1, keepdims=True)
        centered = attended - mean
        square = jnp.sum(centered * centered, axis=1, keepdims=True)
        flow = term_dot(centered * scales[head : head + 1, :], weights[head]).astype(bf16)
        for tile in range(blocks):
            rows = slice(tile * HD, (tile + 1) * HD)
            flows.append(flow[rows])
            both = [
                jnp.sum(jnp.where(on_diagonal, value[rows], 0.0), axis=0, keepdims=True)
                for value in (mean, square)
            ]
            stats.append(terms(jnp.concatenate(both, axis=0)))

    def put(pick):
        for tile in range(TOKENS // HD):
            other = pick(tile)
            rows = jnp.concatenate([flows[tile], flows[other]], axis=1)
            both = jnp.concatenate(
                [stats[tile].astype(f32), stats[other].astype(f32), jnp.zeros((8, HD), f32)],
                axis=0,
            ).astype(bf16)
            for zl in range(ZL):
                send[tile * ZL + zl, 0:ROWS, :] = rows[zl * ROWS : (zl + 1) * ROWS, :]
                send[tile * ZL + zl, ROWS : ROWS + 16, :] = both

    @pl.when(place[1] == 0)
    def _():
        put(lambda tile: blocks + tile)

    @pl.when(place[1] == 1)
    def _():
        put(lambda tile: blocks + tile // ZH)


def sigma_at(index):
    remaining = 1.0 - index.astype(f32) / STEPS
    return flow_shift * remaining / (1.0 + (flow_shift - 1.0) * remaining)


def final_kernel(step, place, got, means, shifts, latents, velocity, advanced, columns):
    zh, zl = place[0], place[2]

    def flows(source):
        return got[source, 0:ROWS, :].astype(f32)

    lower = sum(flows(source) for source in range(Z))
    upper = sum(flows(Z + source) for source in range(Z))
    shared = sum(flows(Z + zh * ZL + source) for source in range(ZL))
    upper = upper[:, :C] + shared[:, C:]
    total = lower + jnp.concatenate([upper, jnp.zeros((ROWS, C), f32)], axis=1)

    table = []
    for source in range(CORE * Z):
        block = got[source, ROWS : ROWS + 16, :].astype(f32)[:8]
        table.append(block + jnp.concatenate([block[2:], block[:2]], axis=0))
    table = jnp.concatenate(table, axis=0)
    row = lax.broadcasted_iota(jnp.int32, (HD, HD), 0)
    kind, source = row & 7, row >> 3
    second = (source >= Z + zh * ZL) & (source < Z + zh * ZL + ZL)

    def gathered(count, of_mean, of_square):
        mean = jnp.sum(jnp.where(of_mean, table, 0.0), axis=0, keepdims=True) / count
        apart = jnp.where(of_mean, table - mean, 0.0)
        spread = jnp.where(of_square, table, 0.0) + HD * (apart * apart)
        spread = jnp.sum(spread, axis=0, keepdims=True) / (count * HD)
        return apart, lax.rsqrt(spread + epsilon)

    main, main_shrink = gathered(
        20, (kind == 0) | ((kind == 4) & second), (kind == 1) | ((kind == 5) & second)
    )
    guide, guide_shrink = gathered(8, (kind == 4) & (source < Z), (kind == 5) & (source < Z))
    block = main + guide
    block = jnp.where(row == 2, main_shrink, jnp.where(row == 3, guide_shrink, block))
    columns[...] = jnp.transpose(block)
    mine = columns[pl.ds(pl.multiple_of(zl * ROWS, ROWS), ROWS), :]
    lane = lax.broadcasted_iota(jnp.int32, (ROWS, HD), 1)
    shrink = jnp.where(lane < C, mine[:, 2:3], mine[:, 3:4])
    high = means[...].astype(bf16)
    moved = term_dot(mine, high) + jnp.dot(
        mine.astype(bf16), (means[...] - high.astype(f32)).astype(bf16), preferred_element_type=f32
    )
    flow = shrink * (total + moved) + shifts[0:1, :]
    main_flow, guide_flow = flow[:, :C], flow[:, C:]
    result = guide_flow + guidance * (main_flow - guide_flow)
    now = jnp.full((1, 1), step[0], jnp.int32)
    velocity[0] = result
    advanced[0] = latents[0] + (sigma_at(now + 1) - sigma_at(now)) * result


def plane_shift(array, by, axis_of_core):
    pairs = []
    for x in range(X):
        for y in range(Y):
            for core in range(CORE):
                if axis_of_core[core] == "x":
                    to = ((x + by) % X, y)
                else:
                    to = (x, (y + by) % Y)
                pairs.append(((x * Y + y) * CORE + core, (to[0] * Y + to[1]) * CORE + core))
    return lax.ppermute(array, ("x", "y", "core"), pairs)


SHIFTS = (-1, 1, 2)


def attend(queries, pairs):
    rows, tiles = HEADS * TOKENS, HEADS * TOKENS // TILE
    return pl.pallas_call(
        attend_kernel,
        out_shape=shape(rows + STAT, HD),
        in_specs=[VMEM] * (1 + SIDE),
        out_specs=VMEM,
        scratch_shapes=[
            pltpu.VMEM((HEADS, KEYS, 2 * HD), bf16),
            pltpu.VMEM((tiles, TILE, KEYS), f32),
            pltpu.VMEM((tiles, TILE, KEYS), bf16),
            pltpu.VMEM((8, HD), f32),
        ],
        compiler_params=params(32),
        cost_estimate=pl.CostEstimate(
            flops=4 * rows * KEYS * HD,
            bytes_accessed=4 * HEADS * KEYS * HD,
            transcendentals=rows * KEYS,
        ),
        name="attend",
    )(queries, *pairs)


def on_device(
    main_query,
    main_key,
    main_value,
    guide_query,
    guide_key,
    guide_value,
    latents,
    step_index,
    main_mod,
    guide_mod,
    main_head,
    guide_head,
):
    place = jnp.stack([lax.axis_index(name) for name in ("zh", "core", "zl")]).astype(jnp.int32)
    guide_send, guide_own = pl.pallas_call(
        pack_guide_kernel,
        out_shape=(shape(3, BLOCK, HD),) * 2,
        in_specs=[SMEM] + [ANY] * 3,
        out_specs=(VMEM,) * 2,
        scratch_shapes=[pltpu.SemaphoreType.DMA((6,))],
        compiler_params=params(16),
        name="pack_guide",
    )(place, guide_query, guide_key, guide_value)
    send = pl.pallas_call(
        pack_kernel,
        out_shape=shape(Z, 9, ROWS, HD),
        in_specs=[ANY] * 3,
        out_specs=VMEM,
        scratch_shapes=[
            pltpu.VMEM((3, ROWS, 20 * HD), bf16),
            pltpu.SemaphoreType.DMA((3,)),
        ],
        compiler_params=params(60),
        name="pack",
    )(main_query, main_key, main_value)
    whole = lambda *dims: pl.BlockSpec(dims, lambda i, step, place: (0,) * len(dims))
    row = lambda *dims: pl.BlockSpec(dims, lambda i, step, place: (step[0], 0, 0))
    weights, scales, means, shifts = pl.pallas_call(
        prepare_kernel,
        out_shape=(
            shape(HEADS, HD, C),
            shape(8, HD, dtype=f32),
            shape(HD, HD, dtype=f32),
            shape(8, HD, dtype=f32),
        ),
        grid_spec=pltpu.PrefetchScalarGridSpec(
            num_scalar_prefetch=2,
            grid=(1,),
            in_specs=[
                row(1, 2, 20 * HD),
                row(1, 2, 8 * HD),
                whole(20 * HD, C),
                whole(8 * HD, C),
            ],
            out_specs=[whole(HEADS, HD, C), whole(8, HD), whole(HD, HD), whole(8, HD)],
        ),
        compiler_params=params(16),
        name="prepare",
    )(step_index, place, main_mod, guide_mod, main_head, guide_head)
    halves = ("zh", "core")
    guide_core = lax.ppermute(guide_own, halves, [(1, 0), (3, 2)])
    guide_half = lax.ppermute(guide_send, halves, [(0, 2), (2, 0)])
    guide_across = lax.ppermute(guide_send, halves, [(1, 2), (3, 0)])
    got = lax.all_to_all(send, ("zh", "zl"), split_axis=0, concat_axis=0, tiled=True)
    got, guide_core, guide_half, guide_across, weights, scales, means, shifts = (
        lax.optimization_barrier(
            (got, guide_core, guide_half, guide_across, weights, scales, means, shifts)
        )
    )
    sibling = lax.ppermute(got, "core", [(0, 1), (1, 0)])
    queries, pairs = pl.pallas_call(
        unpack_kernel,
        out_shape=(shape(HEADS * TOKENS, HD), shape(2 * HEADS, TOKENS, HD)),
        in_specs=[SMEM] + [VMEM] * 6,
        out_specs=(VMEM,) * 2,
        compiler_params=params(16),
        name="unpack",
    )(place, got, sibling, guide_own, guide_core, guide_half, guide_across)
    all_queries = [queries] + [plane_shift(queries, by, "xy") for by in SHIFTS]
    all_pairs = [pairs] + [plane_shift(pairs, by, "yx") for by in SHIFTS]
    parts = [attend(q, all_pairs) for q in all_queries]
    parts[1:] = [plane_shift(p, -by, "xy") for p, by in zip(parts[1:], SHIFTS)]
    send = pl.pallas_call(
        combine_kernel,
        out_shape=shape(CORE * Z, ROWS + 16, HD),
        in_specs=[SMEM] + [VMEM] * (2 + SIDE),
        out_specs=VMEM,
        compiler_params=params(16),
        name="combine",
    )(place, weights, scales, *parts)
    got = lax.all_to_all(send, ("core", "zh", "zl"), split_axis=0, concat_axis=0, tiled=True)
    velocity, advanced = pl.pallas_call(
        final_kernel,
        out_shape=(shape(1, ROWS, C, dtype=f32),) * 2,
        in_specs=[SMEM] * 2 + [VMEM] * 4,
        out_specs=(VMEM,) * 2,
        scratch_shapes=[pltpu.VMEM((HD, HD), f32)],
        compiler_params=params(16),
        name="final",
    )(step_index, place, got, means, shifts, latents)
    return velocity, advanced


def solution(mesh):
    fine = Mesh(mesh.devices.reshape(ZL, X, Y, ZH, CORE), ("zl", "x", "y", "zh", "core"))
    seq = ("x", "y", "zh", "core")
    return jax.shard_map(
        on_device,
        mesh=fine,
        in_specs=(P(seq, "zl", None),) * 3
        + (P(seq, None, "zl"),) * 3
        + (P(seq, "zl", None),)
        + (P(),) * 5,
        out_specs=(P(seq, "zl", None),) * 2,
        check_vma=False,
    )
```

```python
import math

import jax
import jax.numpy as jnp
from jax import lax
from jax.experimental import pallas as pl
from jax.experimental.pallas import tpu as pltpu
from jax.sharding import Mesh, PartitionSpec as P

HD = 128
C = 64
STEPS = 50
ZL, X, Y, ZH, CORE = 4, 4, 4, 2, 2
Z = ZL * ZH
SIDE = 4
ROWS = 32
BLOCK = 128
COLUMN = ROWS * Z
TOKENS = COLUMN * CORE
TILE = 256
HEADS = 2
STAT = 32
KEYS = SIDE * TOKENS

guidance = 2.5
flow_shift = 3.0
epsilon = 1e-06
score_scale = math.log2(math.e) / math.sqrt(HD)

f32 = jnp.float32
bf16 = jnp.bfloat16
VMEM = pl.BlockSpec(memory_space=pltpu.VMEM)
SMEM = pl.BlockSpec(memory_space=pltpu.SMEM)
ANY = pl.BlockSpec(memory_space=pl.ANY)


def shape(*dims, dtype=bf16):
    return jax.ShapeDtypeStruct(dims, dtype)


def params(mib):
    return pltpu.CompilerParams(vmem_limit_bytes=mib * 1024 * 1024)


def pack_guide_kernel(place, gq, gk, gv, send, own, sems):
    copies = []
    for head, to in ((1 - place[0], send), (place[0], own)):
        lanes = pl.ds(pl.multiple_of(head * HD, HD), HD)
        for kind, ref in enumerate((gq, gk, gv)):
            copy = pltpu.make_async_copy(ref.at[0, :, lanes], to.at[kind], sems.at[len(copies)])
            copy.start()
            copies.append(copy)
    for copy in copies:
        copy.wait()


def pack_kernel(mq, mk, mv, send, main, sems):
    copies = []
    for kind, ref in enumerate((mq, mk, mv)):
        copy = pltpu.make_async_copy(ref.at[0], main.at[kind], sems.at[kind])
        copy.start()
        copies.append(copy)
    for kind, copy in enumerate(copies):
        copy.wait()
        for zh_to in range(ZH):
            for zl_to in range(ZL):
                for slot in range(3):
                    head = zl_to * 5 + (4 if slot == 2 else 2 * zh_to + slot)
                    lanes = slice(head * HD, (head + 1) * HD)
                    send[zh_to * ZL + zl_to, slot * 3 + kind] = main[kind, :, lanes]


def unpack_kernel(
    place, got, sibling, guide_own, guide_core, guide_half, guide_across, queries, pairs
):
    zh, core = place[0], place[1]
    for ref, whose in ((got, core), (sibling, 1 - core)):
        base = whose * COLUMN
        for source in range(Z):
            rows = pl.ds(pl.multiple_of(base + source * ROWS, ROWS), ROWS)
            queries[rows, :] = ref[source, core * 3]
            for kind in range(2):
                pairs[kind, rows, :] = ref[source, core * 3 + 1 + kind]

    @pl.when(core == 0)
    def _():
        for ref, zh_from, core_from in (
            (guide_own, zh, 0),
            (guide_core, zh, 1),
            (guide_half, 1 - zh, 0),
            (guide_across, 1 - zh, 1),
        ):
            at = pl.multiple_of(core_from * COLUMN + zh_from * BLOCK, BLOCK)
            queries[pl.ds(pl.multiple_of(TOKENS + at, BLOCK), BLOCK), :] = ref[0]
            pairs[2, pl.ds(at, BLOCK), :] = ref[1]
            pairs[3, pl.ds(at, BLOCK), :] = ref[2]

    @pl.when(core == 1)
    def _():
        for ref, whose in ((got, 1), (sibling, 0)):
            for source in range(Z):
                rows = pl.ds(whose * COLUMN + source * ROWS, ROWS)
                for kind in range(2):
                    pairs[2 + kind, rows, :] = ref[source, 7 + kind]
            for zl in range(ZL):
                rows = pl.ds(TOKENS + whose * BLOCK + zl * ROWS, ROWS)
                queries[rows, :] = ref[zh * ZL + zl, 6]
        queries[pl.ds(TOKENS + COLUMN, COLUMN), :] = jnp.zeros((COLUMN, HD), bf16)


def diagonal():
    return lax.broadcasted_iota(jnp.int32, (HD, HD), 0) == lax.broadcasted_iota(
        jnp.int32, (HD, HD), 1
    )


def attend_kernel(queries, *refs):
    pairs, out = refs[:SIDE], refs[SIDE]
    values, scores, weights, stats = refs[SIDE + 1 :]
    for head in range(HEADS):
        for piece in range(SIDE):
            rows = pl.ds(piece * TOKENS, TOKENS)
            values[head, rows, :HD] = pairs[piece][head * 2 + 1]
            values[head, rows, HD:] = jnp.ones((TOKENS, HD), bf16)
    on_diagonal = diagonal()
    parts = [(piece, half) for piece in range(SIDE) for half in range(TOKENS // TILE)]
    tiles = range(HEADS * TOKENS // TILE)
    tops = []
    for tile in tiles:
        head = tile * TILE // TOKENS
        query = queries[tile * TILE : (tile + 1) * TILE, :]
        highest = None
        for index, (piece, half) in enumerate(parts):
            part = lax.dot_general(
                query,
                pairs[piece][head * 2, half * TILE : (half + 1) * TILE, :],
                (((1,), (1,)), ((), ())),
                preferred_element_type=f32,
            )
            scores[tile, :, index * TILE : (index + 1) * TILE] = part
            here = jnp.maximum(part[:, :HD], part[:, HD:])
            highest = here if highest is None else jnp.maximum(highest, here)
        tops.append(jnp.max(highest, axis=1, keepdims=True) * score_scale)
    for tile in tiles:
        for index in range(len(parts)):
            columns = slice(index * TILE, (index + 1) * TILE)
            part = scores[tile, :, columns]
            weights[tile, :, columns] = jnp.exp2(part * score_scale - tops[tile]).astype(bf16)
    for tile in tiles:
        total = jnp.dot(
            weights[tile], values[tile * TILE // TOKENS], preferred_element_type=f32
        )
        weight_sum = total[:, HD:]
        out[tile * TILE : (tile + 1) * TILE, :] = (total[:, :HD] / weight_sum).astype(bf16)
        level = tops[tile] + jnp.log2(weight_sum)
        for part in range(TILE // HD):
            block = level[part * HD : (part + 1) * HD, :]
            row = jnp.sum(jnp.where(on_diagonal, block, 0.0), axis=0, keepdims=True)
            stats[tile * (TILE // HD) + part : tile * (TILE // HD) + part + 1, :] = row
    level = stats[...]
    high = level.astype(bf16).astype(f32)
    middle = (level - high).astype(bf16).astype(f32)
    low = level - high - middle
    block = jnp.concatenate([high, middle, low, jnp.zeros_like(low)], axis=0)
    out[HEADS * TOKENS :, :] = block.astype(bf16)


def terms(value):
    high = value.astype(bf16)
    low = (value - high.astype(f32)).astype(bf16)
    return jnp.concatenate([high, low], axis=0)


def term_dot(value, weight):
    both = jnp.dot(terms(value), weight, preferred_element_type=f32)
    return both[: value.shape[0]] + both[value.shape[0] :]


def prepare_kernel(
    step, place, main_mod, guide_mod, main_head, guide_head, weights, scales, means, shifts
):
    zh, core, zl = place[0], place[1], place[2]
    first = pl.ds(pl.multiple_of((zl * 5 + 2 * zh + core) * HD, HD), HD)
    shared = pl.ds(pl.multiple_of((zl * 5 + 4) * HD, HD), HD)
    guide = pl.ds(pl.multiple_of((zl * 2 + zh) * HD, HD), HD)
    weights[0] = main_head[first, :]
    scales[...] = jnp.zeros_like(scales)
    scales[0:1, :] = 1.0 + main_mod[0, :, first][1:2].astype(f32)

    @pl.when(core == 0)
    def _():
        weights[1] = guide_head[guide, :]
        scales[1:2, :] = 1.0 + guide_mod[0, :, guide][1:2].astype(f32)

    @pl.when(core == 1)
    def _():
        weights[1] = main_head[shared, :]
        scales[1:2, :] = 1.0 + main_mod[0, :, shared][1:2].astype(f32)

    def rows_of(table, order):
        shift, scale = table[0, 0:1, :].astype(f32), 1.0 + table[0, 1:2, :].astype(f32)
        owner = lax.broadcasted_iota(jnp.int32, scale.shape, 1) >> 7
        rows = [jnp.where(owner == head, scale, 0.0) for head in order] + [shift]
        rows += [jnp.zeros_like(shift)] * (-len(rows) % 8)
        return jnp.concatenate(rows, axis=0)

    main_order = [
        zl * 5 + 2 * zh + core for core in range(CORE) for zh in range(ZH) for zl in range(ZL)
    ] + [zl * 5 + 4 for zl in range(ZL)]
    guide_order = [zl * 2 + zh for zh in range(ZH) for zl in range(ZL)]
    main_rows = term_dot(rows_of(main_mod, main_order), main_head[...])
    guide_rows = term_dot(rows_of(guide_mod, guide_order), guide_head[...])
    main_rows = jnp.concatenate([main_rows, jnp.zeros_like(main_rows)], axis=1)
    guide_rows = jnp.concatenate([jnp.zeros_like(guide_rows), guide_rows], axis=1)
    means[...] = jnp.zeros_like(means)
    for source in range(CORE * Z):
        means[source * 8 : source * 8 + 1, :] = main_rows[source : source + 1]
    for source in range(Z):
        means[source * 8 + 4 : source * 8 + 5, :] = guide_rows[source : source + 1]
        at = (Z + source) * 8 + 4
        means[at : at + 1, :] = main_rows[2 * Z + source % ZL : 2 * Z + source % ZL + 1]
    shifts[...] = jnp.zeros_like(shifts)
    shifts[0:1, :] = main_rows[20:21] + guide_rows[8:9]


def levels_of(part):
    block = part[HEADS * TOKENS :, :].astype(f32)
    return block[0:8] + block[8:16] + block[16:24]


def merge(parts, levels):
    top = levels[0]
    for level in levels[1:]:
        top = jnp.maximum(top, level)
    shares = [jnp.exp2(level - top) for level in levels]
    whole = sum(shares)
    filler = jnp.zeros((HD - 8, HD), f32)
    shares = [jnp.transpose(jnp.concatenate([share / whole, filler], axis=0)) for share in shares]
    tiles = []
    for tile in range(HEADS * TOKENS // HD):
        rows = slice(tile * HD, (tile + 1) * HD)
        tiles.append(
            sum(
                part[rows, :].astype(f32) * share[:, tile : tile + 1]
                for part, share in zip(parts, shares)
            )
        )
    return tiles, top + jnp.log2(whole)


def merge_kernel(*refs):
    parts, result, level = refs[:-2], refs[-2], refs[-1]
    tiles, level[...] = merge(parts, [levels_of(part) for part in parts])
    for tile, value in enumerate(tiles):
        result[tile * HD : (tile + 1) * HD, :] = value


def combine_kernel(place, weights, scales, former, former_level, part, send):
    on_diagonal = diagonal()
    tiles, unused = merge([former, part], [former_level[...], levels_of(part)])
    blocks = TOKENS // HD
    flows, stats = [], []
    for head in range(HEADS):
        attended = jnp.concatenate(tiles[head * blocks : (head + 1) * blocks], axis=0).astype(bf16)
        mean = jnp.mean(attended.astype(f32), axis=1, keepdims=True)
        centered = attended.astype(f32) - mean
        square = jnp.sum(centered * centered, axis=1, keepdims=True)
        flow = term_dot(centered * scales[head : head + 1, :], weights[head]).astype(bf16)
        for tile in range(blocks):
            rows = slice(tile * HD, (tile + 1) * HD)
            flows.append(flow[rows])
            both = [
                jnp.sum(jnp.where(on_diagonal, value[rows], 0.0), axis=0, keepdims=True)
                for value in (mean, square)
            ]
            stats.append(terms(jnp.concatenate(both, axis=0)))

    def put(pick):
        for tile in range(TOKENS // HD):
            other = pick(tile)
            rows = jnp.concatenate([flows[tile], flows[other]], axis=1)
            both = jnp.concatenate(
                [stats[tile].astype(f32), stats[other].astype(f32), jnp.zeros((8, HD), f32)],
                axis=0,
            ).astype(bf16)
            for zl in range(ZL):
                send[tile * ZL + zl, 0:ROWS, :] = rows[zl * ROWS : (zl + 1) * ROWS, :]
                send[tile * ZL + zl, ROWS : ROWS + 16, :] = both

    @pl.when(place[1] == 0)
    def _():
        put(lambda tile: blocks + tile)

    @pl.when(place[1] == 1)
    def _():
        put(lambda tile: blocks + tile // ZH)


def sigma_at(index):
    remaining = 1.0 - index.astype(f32) / STEPS
    return flow_shift * remaining / (1.0 + (flow_shift - 1.0) * remaining)


def final_kernel(step, place, got, means, shifts, latents, velocity, advanced, columns):
    zh, zl = place[0], place[2]

    def flows(source):
        return got[source, 0:ROWS, :].astype(f32)

    lower = sum(flows(source) for source in range(Z))
    upper = sum(flows(Z + source) for source in range(Z))
    shared = sum(flows(Z + zh * ZL + source) for source in range(ZL))
    upper = upper[:, :C] + shared[:, C:]
    total = lower + jnp.concatenate([upper, jnp.zeros((ROWS, C), f32)], axis=1)

    table = []
    for source in range(CORE * Z):
        block = got[source, ROWS : ROWS + 16, :].astype(f32)[:8]
        table.append(block + jnp.concatenate([block[2:], block[:2]], axis=0))
    table = jnp.concatenate(table, axis=0)
    row = lax.broadcasted_iota(jnp.int32, (HD, HD), 0)
    kind, source = row & 7, row >> 3
    second = (source >= Z + zh * ZL) & (source < Z + zh * ZL + ZL)

    def gathered(count, of_mean, of_square):
        mean = jnp.sum(jnp.where(of_mean, table, 0.0), axis=0, keepdims=True) / count
        apart = jnp.where(of_mean, table - mean, 0.0)
        spread = jnp.where(of_square, table, 0.0) + HD * (apart * apart)
        spread = jnp.sum(spread, axis=0, keepdims=True) / (count * HD)
        return apart, lax.rsqrt(spread + epsilon)

    main, main_shrink = gathered(
        20, (kind == 0) | ((kind == 4) & second), (kind == 1) | ((kind == 5) & second)
    )
    guide, guide_shrink = gathered(8, (kind == 4) & (source < Z), (kind == 5) & (source < Z))
    block = main + guide
    block = jnp.where(row == 2, main_shrink, jnp.where(row == 3, guide_shrink, block))
    columns[...] = jnp.transpose(block)
    mine = columns[pl.ds(pl.multiple_of(zl * ROWS, ROWS), ROWS), :]
    lane = lax.broadcasted_iota(jnp.int32, (ROWS, HD), 1)
    shrink = jnp.where(lane < C, mine[:, 2:3], mine[:, 3:4])
    high = means[...].astype(bf16)
    moved = term_dot(mine, high) + jnp.dot(
        mine.astype(bf16), (means[...] - high.astype(f32)).astype(bf16), preferred_element_type=f32
    )
    flow = shrink * (total + moved) + shifts[0:1, :]
    main_flow, guide_flow = flow[:, :C], flow[:, C:]
    result = guide_flow + guidance * (main_flow - guide_flow)
    now = jnp.full((1, 1), step[0], jnp.int32)
    velocity[0] = result
    advanced[0] = latents[0] + (sigma_at(now + 1) - sigma_at(now)) * result


def plane_shift(array, by, axis_of_core):
    pairs = []
    for x in range(X):
        for y in range(Y):
            for core in range(CORE):
                if axis_of_core[core] == "x":
                    to = ((x + by) % X, y)
                else:
                    to = (x, (y + by) % Y)
                pairs.append(((x * Y + y) * CORE + core, (to[0] * Y + to[1]) * CORE + core))
    return lax.ppermute(array, ("x", "y", "core"), pairs)


SHIFTS = (-1, 1, 2)


def attend(queries, pairs):
    rows, tiles = HEADS * TOKENS, HEADS * TOKENS // TILE
    return pl.pallas_call(
        attend_kernel,
        out_shape=shape(rows + STAT, HD),
        in_specs=[VMEM] * (1 + SIDE),
        out_specs=VMEM,
        scratch_shapes=[
            pltpu.VMEM((HEADS, KEYS, 2 * HD), bf16),
            pltpu.VMEM((tiles, TILE, KEYS), f32),
            pltpu.VMEM((tiles, TILE, KEYS), bf16),
            pltpu.VMEM((8, HD), f32),
        ],
        compiler_params=params(32),
        cost_estimate=pl.CostEstimate(
            flops=4 * rows * KEYS * HD,
            bytes_accessed=4 * HEADS * KEYS * HD,
            transcendentals=rows * KEYS,
        ),
        name="attend",
    )(queries, *pairs)


def on_device(
    main_query,
    main_key,
    main_value,
    guide_query,
    guide_key,
    guide_value,
    latents,
    step_index,
    main_mod,
    guide_mod,
    main_head,
    guide_head,
):
    place = jnp.stack([lax.axis_index(name) for name in ("zh", "core", "zl")]).astype(jnp.int32)
    guide_send, guide_own = pl.pallas_call(
        pack_guide_kernel,
        out_shape=(shape(3, BLOCK, HD),) * 2,
        in_specs=[SMEM] + [ANY] * 3,
        out_specs=(VMEM,) * 2,
        scratch_shapes=[pltpu.SemaphoreType.DMA((6,))],
        compiler_params=params(16),
        name="pack_guide",
    )(place, guide_query, guide_key, guide_value)
    send = pl.pallas_call(
        pack_kernel,
        out_shape=shape(Z, 9, ROWS, HD),
        in_specs=[ANY] * 3,
        out_specs=VMEM,
        scratch_shapes=[
            pltpu.VMEM((3, ROWS, 20 * HD), bf16),
            pltpu.SemaphoreType.DMA((3,)),
        ],
        compiler_params=params(60),
        name="pack",
    )(main_query, main_key, main_value)
    whole = lambda *dims: pl.BlockSpec(dims, lambda i, step, place: (0,) * len(dims))
    row = lambda *dims: pl.BlockSpec(dims, lambda i, step, place: (step[0], 0, 0))
    weights, scales, means, shifts = pl.pallas_call(
        prepare_kernel,
        out_shape=(
            shape(HEADS, HD, C),
            shape(8, HD, dtype=f32),
            shape(HD, HD, dtype=f32),
            shape(8, HD, dtype=f32),
        ),
        grid_spec=pltpu.PrefetchScalarGridSpec(
            num_scalar_prefetch=2,
            grid=(1,),
            in_specs=[
                row(1, 2, 20 * HD),
                row(1, 2, 8 * HD),
                whole(20 * HD, C),
                whole(8 * HD, C),
            ],
            out_specs=[whole(HEADS, HD, C), whole(8, HD), whole(HD, HD), whole(8, HD)],
        ),
        compiler_params=params(16),
        name="prepare",
    )(step_index, place, main_mod, guide_mod, main_head, guide_head)
    halves = ("zh", "core")
    guide_core = lax.ppermute(guide_own, halves, [(1, 0), (3, 2)])
    guide_half = lax.ppermute(guide_send, halves, [(0, 2), (2, 0)])
    guide_across = lax.ppermute(guide_send, halves, [(1, 2), (3, 0)])
    got = lax.all_to_all(send, ("zh", "zl"), split_axis=0, concat_axis=0, tiled=True)
    got, guide_core, guide_half, guide_across, weights, scales, means, shifts = (
        lax.optimization_barrier(
            (got, guide_core, guide_half, guide_across, weights, scales, means, shifts)
        )
    )
    sibling = lax.ppermute(got, "core", [(0, 1), (1, 0)])
    queries, pairs = pl.pallas_call(
        unpack_kernel,
        out_shape=(shape(HEADS * TOKENS, HD), shape(2 * HEADS, TOKENS, HD)),
        in_specs=[SMEM] + [VMEM] * 6,
        out_specs=(VMEM,) * 2,
        compiler_params=params(16),
        name="unpack",
    )(place, got, sibling, guide_own, guide_core, guide_half, guide_across)
    all_queries = [queries] + [plane_shift(queries, by, "xy") for by in SHIFTS]
    all_pairs = [pairs] + [plane_shift(pairs, by, "yx") for by in SHIFTS]
    parts = [attend(q, all_pairs) for q in all_queries]
    parts[1:] = [plane_shift(p, -by, "xy") for p, by in zip(parts[1:], SHIFTS)]
    former, level = pl.pallas_call(
        merge_kernel,
        out_shape=(shape(HEADS * TOKENS, HD, dtype=f32), shape(8, HD, dtype=f32)),
        in_specs=[VMEM] * (SIDE - 1),
        out_specs=(VMEM,) * 2,
        compiler_params=params(16),
        name="merge",
    )(*parts[:-1])
    send = pl.pallas_call(
        combine_kernel,
        out_shape=shape(CORE * Z, ROWS + 16, HD),
        in_specs=[SMEM] + [VMEM] * 5,
        out_specs=VMEM,
        compiler_params=params(16),
        name="combine",
    )(place, weights, scales, former, level, parts[-1])
    got = lax.all_to_all(send, ("core", "zh", "zl"), split_axis=0, concat_axis=0, tiled=True)
    velocity, advanced = pl.pallas_call(
        final_kernel,
        out_shape=(shape(1, ROWS, C, dtype=f32),) * 2,
        in_specs=[SMEM] * 2 + [VMEM] * 4,
        out_specs=(VMEM,) * 2,
        scratch_shapes=[pltpu.VMEM((HD, HD), f32)],
        compiler_params=params(16),
        name="final",
    )(step_index, place, got, means, shifts, latents)
    return velocity, advanced


def solution(mesh):
    fine = Mesh(mesh.devices.reshape(ZL, X, Y, ZH, CORE), ("zl", "x", "y", "zh", "core"))
    seq = ("x", "y", "zh", "core")
    return jax.shard_map(
        on_device,
        mesh=fine,
        in_specs=(P(seq, "zl", None),) * 3
        + (P(seq, None, "zl"),) * 3
        + (P(seq, "zl", None),)
        + (P(),) * 5,
        out_specs=(P(seq, "zl", None),) * 2,
        check_vma=False,
    )
```

```python
import math

import jax
import jax.numpy as jnp
from jax import lax
from jax.experimental import pallas as pl
from jax.experimental.pallas import tpu as pltpu
from jax.sharding import Mesh, PartitionSpec as P

HD = 128
C = 64
STEPS = 50
ZL, X, Y, ZH, CORE = 4, 4, 4, 2, 2
Z = ZL * ZH
SIDE = 4
ROWS = 32
PART = ROWS // ZH
SET = 3 * ROWS
MESSAGE = 2 * SET + 2 * ROWS + PART
BLOCK = 128
COLUMN = ROWS * Z
TOKENS = COLUMN * CORE
TILE = 256
HEADS = 2
STAT = 32
KEYS = SIDE * TOKENS

guidance = 2.5
flow_shift = 3.0
epsilon = 1e-06
score_scale = math.log2(math.e) / math.sqrt(HD)

f32 = jnp.float32
bf16 = jnp.bfloat16
VMEM = pl.BlockSpec(memory_space=pltpu.VMEM)
SMEM = pl.BlockSpec(memory_space=pltpu.SMEM)
ANY = pl.BlockSpec(memory_space=pl.ANY)


def shape(*dims, dtype=bf16):
    return jax.ShapeDtypeStruct(dims, dtype)


def params(mib):
    return pltpu.CompilerParams(vmem_limit_bytes=mib * 1024 * 1024)


def pack_guide_kernel(place, gq, gk, gv, send, own, sems):
    copies = []
    for head, to in ((1 - place[0], send), (place[0], own)):
        lanes = pl.ds(pl.multiple_of(head * HD, HD), HD)
        for kind, ref in enumerate((gq, gk, gv)):
            copy = pltpu.make_async_copy(ref.at[0, :, lanes], to.at[kind], sems.at[len(copies)])
            copy.start()
            copies.append(copy)
    for copy in copies:
        copy.wait()


def pack_kernel(mq, mk, mv, send, main, sems):
    copies = []
    for kind, ref in enumerate((mq, mk, mv)):
        copy = pltpu.make_async_copy(ref.at[0], main.at[kind], sems.at[kind])
        copy.start()
        copies.append(copy)
    for kind, copy in enumerate(copies):
        copy.wait()
        for zh_to in range(ZH):
            for zl_to in range(ZL):
                to = zh_to * ZL + zl_to
                for slot in range(2):
                    head = zl_to * 5 + 2 * zh_to + slot
                    start = slot * SET + kind * ROWS
                    send[to, start : start + ROWS, :] = main[kind, :, head * HD : (head + 1) * HD]
                lanes = slice((zl_to * 5 + 4) * HD, (zl_to * 5 + 5) * HD)
                if kind == 0:
                    rows = slice(zh_to * PART, (zh_to + 1) * PART)
                    send[to, 2 * SET + 2 * ROWS :, :] = main[0, rows, lanes]
                else:
                    start = 2 * SET + (kind - 1) * ROWS
                    send[to, start : start + ROWS, :] = main[kind, :, lanes]


def unpack_kernel(
    place, got, sibling, guide_own, guide_core, guide_half, guide_across, queries, pairs
):
    zh, core = place[0], place[1]
    for ref, whose in ((got, core), (sibling, 1 - core)):
        base = whose * COLUMN
        for source in range(Z):
            rows = pl.ds(pl.multiple_of(base + source * ROWS, ROWS), ROWS)
            start = pl.multiple_of(core * SET, ROWS)
            queries[rows, :] = ref[source, pl.ds(start, ROWS), :]
            for kind in range(2):
                at = pl.multiple_of(start + (1 + kind) * ROWS, ROWS)
                pairs[kind, rows, :] = ref[source, pl.ds(at, ROWS), :]

    @pl.when(core == 0)
    def _():
        for ref, zh_from, core_from in (
            (guide_own, zh, 0),
            (guide_core, zh, 1),
            (guide_half, 1 - zh, 0),
            (guide_across, 1 - zh, 1),
        ):
            at = pl.multiple_of(core_from * COLUMN + zh_from * BLOCK, BLOCK)
            queries[pl.ds(pl.multiple_of(TOKENS + at, BLOCK), BLOCK), :] = ref[0]
            pairs[2, pl.ds(at, BLOCK), :] = ref[1]
            pairs[3, pl.ds(at, BLOCK), :] = ref[2]

    @pl.when(core == 1)
    def _():
        for ref, whose in ((got, 1), (sibling, 0)):
            for source in range(Z):
                rows = pl.ds(whose * COLUMN + source * ROWS, ROWS)
                for kind in range(2):
                    start = 2 * SET + kind * ROWS
                    pairs[2 + kind, rows, :] = ref[source, start : start + ROWS, :]
                rows = pl.ds(TOKENS + whose * BLOCK + source * PART, PART)
                queries[rows, :] = ref[source, 2 * SET + 2 * ROWS :, :]
        queries[pl.ds(TOKENS + COLUMN, COLUMN), :] = jnp.zeros((COLUMN, HD), bf16)


def diagonal():
    return lax.broadcasted_iota(jnp.int32, (HD, HD), 0) == lax.broadcasted_iota(
        jnp.int32, (HD, HD), 1
    )


def attend_kernel(queries, *refs):
    pairs, out = refs[:SIDE], refs[SIDE]
    values, scores, weights, stats = refs[SIDE + 1 :]
    for head in range(HEADS):
        for piece in range(SIDE):
            rows = pl.ds(piece * TOKENS, TOKENS)
            values[head, rows, :HD] = pairs[piece][head * 2 + 1]
            values[head, rows, HD:] = jnp.ones((TOKENS, HD), bf16)
    on_diagonal = diagonal()
    parts = [(piece, half) for piece in range(SIDE) for half in range(TOKENS // TILE)]
    tiles = range(HEADS * TOKENS // TILE)
    tops = []
    for tile in tiles:
        head = tile * TILE // TOKENS
        query = queries[tile * TILE : (tile + 1) * TILE, :]
        highest = None
        for index, (piece, half) in enumerate(parts):
            part = lax.dot_general(
                query,
                pairs[piece][head * 2, half * TILE : (half + 1) * TILE, :],
                (((1,), (1,)), ((), ())),
                preferred_element_type=f32,
            )
            scores[tile, :, index * TILE : (index + 1) * TILE] = part
            here = jnp.maximum(part[:, :HD], part[:, HD:])
            highest = here if highest is None else jnp.maximum(highest, here)
        tops.append(jnp.max(highest, axis=1, keepdims=True) * score_scale)
    for tile in tiles:
        for index in range(len(parts)):
            columns = slice(index * TILE, (index + 1) * TILE)
            part = scores[tile, :, columns]
            weights[tile, :, columns] = jnp.exp2(part * score_scale - tops[tile]).astype(bf16)
    for tile in tiles:
        total = jnp.dot(
            weights[tile], values[tile * TILE // TOKENS], preferred_element_type=f32
        )
        weight_sum = total[:, HD:]
        out[tile * TILE : (tile + 1) * TILE, :] = (total[:, :HD] / weight_sum).astype(bf16)
        level = tops[tile] + jnp.log2(weight_sum)
        for part in range(TILE // HD):
            block = level[part * HD : (part + 1) * HD, :]
            row = jnp.sum(jnp.where(on_diagonal, block, 0.0), axis=0, keepdims=True)
            stats[tile * (TILE // HD) + part : tile * (TILE // HD) + part + 1, :] = row
    level = stats[...]
    high = level.astype(bf16).astype(f32)
    middle = (level - high).astype(bf16).astype(f32)
    low = level - high - middle
    block = jnp.concatenate([high, middle, low, jnp.zeros_like(low)], axis=0)
    out[HEADS * TOKENS :, :] = block.astype(bf16)


def terms(value):
    high = value.astype(bf16)
    low = (value - high.astype(f32)).astype(bf16)
    return jnp.concatenate([high, low], axis=0)


def term_dot(value, weight):
    both = jnp.dot(terms(value), weight, preferred_element_type=f32)
    return both[: value.shape[0]] + both[value.shape[0] :]


def prepare_kernel(
    step, place, main_mod, guide_mod, main_head, guide_head, weights, scales, means, shifts
):
    zh, core, zl = place[0], place[1], place[2]
    first = pl.ds(pl.multiple_of((zl * 5 + 2 * zh + core) * HD, HD), HD)
    shared = pl.ds(pl.multiple_of((zl * 5 + 4) * HD, HD), HD)
    guide = pl.ds(pl.multiple_of((zl * 2 + zh) * HD, HD), HD)
    weights[0] = main_head[first, :]
    scales[...] = jnp.zeros_like(scales)
    scales[0:1, :] = 1.0 + main_mod[0, :, first][1:2].astype(f32)

    @pl.when(core == 0)
    def _():
        weights[1] = guide_head[guide, :]
        scales[1:2, :] = 1.0 + guide_mod[0, :, guide][1:2].astype(f32)

    @pl.when(core == 1)
    def _():
        weights[1] = main_head[shared, :]
        scales[1:2, :] = 1.0 + main_mod[0, :, shared][1:2].astype(f32)

    def rows_of(table, order):
        shift, scale = table[0, 0:1, :].astype(f32), 1.0 + table[0, 1:2, :].astype(f32)
        owner = lax.broadcasted_iota(jnp.int32, scale.shape, 1) >> 7
        rows = [jnp.where(owner == head, scale, 0.0) for head in order] + [shift]
        rows += [jnp.zeros_like(shift)] * (-len(rows) % 8)
        return jnp.concatenate(rows, axis=0)

    main_order = [
        zl * 5 + 2 * zh + core for core in range(CORE) for zh in range(ZH) for zl in range(ZL)
    ] + [zl * 5 + 4 for zl in range(ZL)]
    guide_order = [zl * 2 + zh for zh in range(ZH) for zl in range(ZL)]
    main_rows = term_dot(rows_of(main_mod, main_order), main_head[...])
    guide_rows = term_dot(rows_of(guide_mod, guide_order), guide_head[...])
    main_rows = jnp.concatenate([main_rows, jnp.zeros_like(main_rows)], axis=1)
    guide_rows = jnp.concatenate([jnp.zeros_like(guide_rows), guide_rows], axis=1)
    means[...] = jnp.zeros_like(means)
    for source in range(CORE * Z):
        means[source * 8 : source * 8 + 1, :] = main_rows[source : source + 1]
    for source in range(Z):
        means[source * 8 + 4 : source * 8 + 5, :] = guide_rows[source : source + 1]
        at = (Z + source) * 8 + 4
        means[at : at + 1, :] = main_rows[2 * Z + source % ZL : 2 * Z + source % ZL + 1]
    shifts[...] = jnp.zeros_like(shifts)
    shifts[0:1, :] = main_rows[20:21] + guide_rows[8:9]


def levels_of(part):
    block = part[HEADS * TOKENS :, :].astype(f32)
    return block[0:8] + block[8:16] + block[16:24]


def merge(parts, levels):
    top = levels[0]
    for level in levels[1:]:
        top = jnp.maximum(top, level)
    shares = [jnp.exp2(level - top) for level in levels]
    whole = sum(shares)
    filler = jnp.zeros((HD - 8, HD), f32)
    shares = [jnp.transpose(jnp.concatenate([share / whole, filler], axis=0)) for share in shares]
    tiles = []
    for tile in range(HEADS * TOKENS // HD):
        rows = slice(tile * HD, (tile + 1) * HD)
        tiles.append(
            sum(
                part[rows, :].astype(f32) * share[:, tile : tile + 1]
                for part, share in zip(parts, shares)
            )
        )
    return tiles, top + jnp.log2(whole)


def merge_kernel(*refs):
    parts, result, level = refs[:-2], refs[-2], refs[-1]
    tiles, level[...] = merge(parts, [levels_of(part) for part in parts])
    for tile, value in enumerate(tiles):
        result[tile * HD : (tile + 1) * HD, :] = value


def combine_kernel(place, weights, scales, former, former_level, part, send):
    on_diagonal = diagonal()
    tiles, unused = merge([former, part], [former_level[...], levels_of(part)])
    blocks = TOKENS // HD
    for tile in range(blocks):
        narrow = tiles[blocks + tile // ZH]
        start = tile % ZH * (HD // ZH)
        pieces = []
        for row in range(start, start + HD // ZH, PART):
            pieces += [narrow[row : row + PART]] * ZH
        wide = jnp.concatenate(pieces, axis=0)
        tiles.append(jnp.where(place[1] == 1, wide, tiles[blocks + tile]))
    tiles = tiles[:blocks] + tiles[2 * blocks :]
    flows, stats = [], []
    for head in range(HEADS):
        attended = jnp.concatenate(tiles[head * blocks : (head + 1) * blocks], axis=0).astype(bf16)
        mean = jnp.mean(attended.astype(f32), axis=1, keepdims=True)
        centered = attended.astype(f32) - mean
        square = jnp.sum(centered * centered, axis=1, keepdims=True)
        flow = term_dot(centered * scales[head : head + 1, :], weights[head]).astype(bf16)
        for tile in range(blocks):
            rows = slice(tile * HD, (tile + 1) * HD)
            flows.append(flow[rows])
            both = [
                jnp.sum(jnp.where(on_diagonal, value[rows], 0.0), axis=0, keepdims=True)
                for value in (mean, square)
            ]
            stats.append(terms(jnp.concatenate(both, axis=0)))

    for tile in range(blocks):
        other = blocks + tile
        rows = jnp.concatenate([flows[tile], flows[other]], axis=1)
        both = jnp.concatenate(
            [stats[tile].astype(f32), stats[other].astype(f32), jnp.zeros((8, HD), f32)],
            axis=0,
        ).astype(bf16)
        for zl in range(ZL):
            send[tile * ZL + zl, 0:ROWS, :] = rows[zl * ROWS : (zl + 1) * ROWS, :]
            send[tile * ZL + zl, ROWS : ROWS + 16, :] = both


def sigma_at(index):
    remaining = 1.0 - index.astype(f32) / STEPS
    return flow_shift * remaining / (1.0 + (flow_shift - 1.0) * remaining)


def final_kernel(step, place, got, means, shifts, latents, velocity, advanced, columns):
    zl = place[2]

    def flows(source):
        return got[source, 0:ROWS, :].astype(f32)

    lower = sum(flows(source) for source in range(Z))
    upper = sum(flows(Z + source) for source in range(Z))
    shared = [sum(flows(Z + zh * ZL + zl) for zl in range(ZL)) for zh in range(ZH)]
    shared = jnp.concatenate([shared[0][:PART], shared[1][PART:]], axis=0)
    upper = upper[:, :C] + shared[:, C:]
    total = lower + jnp.concatenate([upper, jnp.zeros((ROWS, C), f32)], axis=1)

    table = []
    for source in range(CORE * Z):
        block = got[source, ROWS : ROWS + 16, :].astype(f32)[:8]
        table.append(block + jnp.concatenate([block[2:], block[:2]], axis=0))
    table = jnp.concatenate(table, axis=0)
    row = lax.broadcasted_iota(jnp.int32, (HD, HD), 0)
    kind, source = row & 7, row >> 3
    token = lax.broadcasted_iota(jnp.int32, (HD, HD), 1)
    second = (source >= Z) & (((source - Z) >> 2) == ((token >> 4) & 1))

    def gathered(count, of_mean, of_square):
        mean = jnp.sum(jnp.where(of_mean, table, 0.0), axis=0, keepdims=True) / count
        apart = jnp.where(of_mean, table - mean, 0.0)
        spread = jnp.where(of_square, table, 0.0) + HD * (apart * apart)
        spread = jnp.sum(spread, axis=0, keepdims=True) / (count * HD)
        return apart, lax.rsqrt(spread + epsilon)

    main, main_shrink = gathered(
        20, (kind == 0) | ((kind == 4) & second), (kind == 1) | ((kind == 5) & second)
    )
    guide, guide_shrink = gathered(8, (kind == 4) & (source < Z), (kind == 5) & (source < Z))
    block = main + guide
    block = jnp.where(row == 2, main_shrink, jnp.where(row == 3, guide_shrink, block))
    columns[...] = jnp.transpose(block)
    mine = columns[pl.ds(pl.multiple_of(zl * ROWS, ROWS), ROWS), :]
    lane = lax.broadcasted_iota(jnp.int32, (ROWS, HD), 1)
    shrink = jnp.where(lane < C, mine[:, 2:3], mine[:, 3:4])
    high = means[...].astype(bf16)
    moved = term_dot(mine, high) + jnp.dot(
        mine.astype(bf16), (means[...] - high.astype(f32)).astype(bf16), preferred_element_type=f32
    )
    flow = shrink * (total + moved) + shifts[0:1, :]
    main_flow, guide_flow = flow[:, :C], flow[:, C:]
    result = guide_flow + guidance * (main_flow - guide_flow)
    now = jnp.full((1, 1), step[0], jnp.int32)
    velocity[0] = result
    advanced[0] = latents[0] + (sigma_at(now + 1) - sigma_at(now)) * result


def plane_shift(array, by, axis_of_core):
    pairs = []
    for x in range(X):
        for y in range(Y):
            for core in range(CORE):
                if axis_of_core[core] == "x":
                    to = ((x + by) % X, y)
                else:
                    to = (x, (y + by) % Y)
                pairs.append(((x * Y + y) * CORE + core, (to[0] * Y + to[1]) * CORE + core))
    return lax.ppermute(array, ("x", "y", "core"), pairs)


SHIFTS = (-1, 1, 2)


def attend(queries, pairs):
    rows, tiles = HEADS * TOKENS, HEADS * TOKENS // TILE
    return pl.pallas_call(
        attend_kernel,
        out_shape=shape(rows + STAT, HD),
        in_specs=[VMEM] * (1 + SIDE),
        out_specs=VMEM,
        scratch_shapes=[
            pltpu.VMEM((HEADS, KEYS, 2 * HD), bf16),
            pltpu.VMEM((tiles, TILE, KEYS), f32),
            pltpu.VMEM((tiles, TILE, KEYS), bf16),
            pltpu.VMEM((8, HD), f32),
        ],
        compiler_params=params(32),
        cost_estimate=pl.CostEstimate(
            flops=4 * rows * KEYS * HD,
            bytes_accessed=4 * HEADS * KEYS * HD,
            transcendentals=rows * KEYS,
        ),
        name="attend",
    )(queries, *pairs)


def on_device(
    main_query,
    main_key,
    main_value,
    guide_query,
    guide_key,
    guide_value,
    latents,
    step_index,
    main_mod,
    guide_mod,
    main_head,
    guide_head,
):
    place = jnp.stack([lax.axis_index(name) for name in ("zh", "core", "zl")]).astype(jnp.int32)
    guide_send, guide_own = pl.pallas_call(
        pack_guide_kernel,
        out_shape=(shape(3, BLOCK, HD),) * 2,
        in_specs=[SMEM] + [ANY] * 3,
        out_specs=(VMEM,) * 2,
        scratch_shapes=[pltpu.SemaphoreType.DMA((6,))],
        compiler_params=params(16),
        name="pack_guide",
    )(place, guide_query, guide_key, guide_value)
    send = pl.pallas_call(
        pack_kernel,
        out_shape=shape(Z, MESSAGE, HD),
        in_specs=[ANY] * 3,
        out_specs=VMEM,
        scratch_shapes=[
            pltpu.VMEM((3, ROWS, 20 * HD), bf16),
            pltpu.SemaphoreType.DMA((3,)),
        ],
        compiler_params=params(60),
        name="pack",
    )(main_query, main_key, main_value)
    whole = lambda *dims: pl.BlockSpec(dims, lambda i, step, place: (0,) * len(dims))
    row = lambda *dims: pl.BlockSpec(dims, lambda i, step, place: (step[0], 0, 0))
    weights, scales, means, shifts = pl.pallas_call(
        prepare_kernel,
        out_shape=(
            shape(HEADS, HD, C),
            shape(8, HD, dtype=f32),
            shape(HD, HD, dtype=f32),
            shape(8, HD, dtype=f32),
        ),
        grid_spec=pltpu.PrefetchScalarGridSpec(
            num_scalar_prefetch=2,
            grid=(1,),
            in_specs=[
                row(1, 2, 20 * HD),
                row(1, 2, 8 * HD),
                whole(20 * HD, C),
                whole(8 * HD, C),
            ],
            out_specs=[whole(HEADS, HD, C), whole(8, HD), whole(HD, HD), whole(8, HD)],
        ),
        compiler_params=params(16),
        name="prepare",
    )(step_index, place, main_mod, guide_mod, main_head, guide_head)
    halves = ("zh", "core")
    guide_core = lax.ppermute(guide_own, halves, [(1, 0), (3, 2)])
    guide_half = lax.ppermute(guide_send, halves, [(0, 2), (2, 0)])
    guide_across = lax.ppermute(guide_send, halves, [(1, 2), (3, 0)])
    got = lax.all_to_all(send, ("zh", "zl"), split_axis=0, concat_axis=0, tiled=True)
    got, guide_core, guide_half, guide_across, weights, scales, means, shifts = (
        lax.optimization_barrier(
            (got, guide_core, guide_half, guide_across, weights, scales, means, shifts)
        )
    )
    sibling = lax.ppermute(got, "core", [(0, 1), (1, 0)])
    queries, pairs = pl.pallas_call(
        unpack_kernel,
        out_shape=(shape(HEADS * TOKENS, HD), shape(2 * HEADS, TOKENS, HD)),
        in_specs=[SMEM] + [VMEM] * 6,
        out_specs=(VMEM,) * 2,
        compiler_params=params(16),
        name="unpack",
    )(place, got, sibling, guide_own, guide_core, guide_half, guide_across)
    all_queries = [queries] + [plane_shift(queries, by, "xy") for by in SHIFTS]
    all_pairs = [pairs] + [plane_shift(pairs, by, "yx") for by in SHIFTS]
    parts = [attend(q, all_pairs) for q in all_queries]
    parts[1:] = [plane_shift(p, -by, "xy") for p, by in zip(parts[1:], SHIFTS)]
    former, level = pl.pallas_call(
        merge_kernel,
        out_shape=(shape(HEADS * TOKENS, HD, dtype=f32), shape(8, HD, dtype=f32)),
        in_specs=[VMEM] * (SIDE - 1),
        out_specs=(VMEM,) * 2,
        compiler_params=params(16),
        name="merge",
    )(*parts[:-1])
    send = pl.pallas_call(
        combine_kernel,
        out_shape=shape(CORE * Z, ROWS + 16, HD),
        in_specs=[SMEM] + [VMEM] * 5,
        out_specs=VMEM,
        compiler_params=params(16),
        name="combine",
    )(place, weights, scales, former, level, parts[-1])
    got = lax.all_to_all(send, ("core", "zh", "zl"), split_axis=0, concat_axis=0, tiled=True)
    velocity, advanced = pl.pallas_call(
        final_kernel,
        out_shape=(shape(1, ROWS, C, dtype=f32),) * 2,
        in_specs=[SMEM] * 2 + [VMEM] * 4,
        out_specs=(VMEM,) * 2,
        scratch_shapes=[pltpu.VMEM((HD, HD), f32)],
        compiler_params=params(16),
        name="final",
    )(step_index, place, got, means, shifts, latents)
    return velocity, advanced


def solution(mesh):
    fine = Mesh(mesh.devices.reshape(ZL, X, Y, ZH, CORE), ("zl", "x", "y", "zh", "core"))
    seq = ("x", "y", "zh", "core")
    return jax.shard_map(
        on_device,
        mesh=fine,
        in_specs=(P(seq, "zl", None),) * 3
        + (P(seq, None, "zl"),) * 3
        + (P(seq, "zl", None),)
        + (P(),) * 5,
        out_specs=(P(seq, "zl", None),) * 2,
        check_vma=False,
    )
```

```python
import math

import jax
import jax.numpy as jnp
from jax import lax
from jax.experimental import pallas as pl
from jax.experimental.pallas import tpu as pltpu
from jax.sharding import Mesh, PartitionSpec as P

HD = 128
C = 64
STEPS = 50
ZL, X, Y, ZH, CORE = 4, 4, 4, 2, 2
Z = ZL * ZH
SIDE = 4
ROWS = 32
PART = ROWS // ZH
SET = 3 * ROWS
MESSAGE = 2 * SET + 2 * ROWS + PART
BLOCK = 128
COLUMN = ROWS * Z
TOKENS = COLUMN * CORE
TILE = 256
HEADS = 2
STAT = 32
KEYS = SIDE * TOKENS

guidance = 2.5
flow_shift = 3.0
epsilon = 1e-06
score_scale = math.log2(math.e) / math.sqrt(HD)

f32 = jnp.float32
bf16 = jnp.bfloat16
VMEM = pl.BlockSpec(memory_space=pltpu.VMEM)
SMEM = pl.BlockSpec(memory_space=pltpu.SMEM)
ANY = pl.BlockSpec(memory_space=pl.ANY)


def shape(*dims, dtype=bf16):
    return jax.ShapeDtypeStruct(dims, dtype)


def params(mib):
    return pltpu.CompilerParams(vmem_limit_bytes=mib * 1024 * 1024)


def pack_guide_kernel(place, gq, gk, gv, send, own, sems):
    copies = []
    for head, to in ((1 - place[0], send), (place[0], own)):
        lanes = pl.ds(pl.multiple_of(head * HD, HD), HD)
        for kind, ref in enumerate((gq, gk, gv)):
            copy = pltpu.make_async_copy(ref.at[0, :, lanes], to.at[kind], sems.at[len(copies)])
            copy.start()
            copies.append(copy)
    for copy in copies:
        copy.wait()


def pack_kernel(mq, mk, mv, send, main, sems):
    copies = []
    for kind, ref in enumerate((mq, mk, mv)):
        copy = pltpu.make_async_copy(ref.at[0], main.at[kind], sems.at[kind])
        copy.start()
        copies.append(copy)
    for kind, copy in enumerate(copies):
        copy.wait()
        for zh_to in range(ZH):
            for zl_to in range(ZL):
                to = zh_to * ZL + zl_to
                for slot in range(2):
                    head = zl_to * 5 + 2 * zh_to + slot
                    start = slot * SET + kind * ROWS
                    send[to, start : start + ROWS, :] = main[kind, :, head * HD : (head + 1) * HD]
                lanes = slice((zl_to * 5 + 4) * HD, (zl_to * 5 + 5) * HD)
                if kind == 0:
                    rows = slice(zh_to * PART, (zh_to + 1) * PART)
                    send[to, 2 * SET + 2 * ROWS :, :] = main[0, rows, lanes]
                else:
                    start = 2 * SET + (kind - 1) * ROWS
                    send[to, start : start + ROWS, :] = main[kind, :, lanes]


def unpack_kernel(
    place, got, sibling, guide_own, guide_core, guide_half, guide_across, queries, pairs
):
    zh, core = place[0], place[1]
    for ref, whose in ((got, core), (sibling, 1 - core)):
        base = whose * COLUMN
        for source in range(Z):
            rows = pl.ds(pl.multiple_of(base + source * ROWS, ROWS), ROWS)
            start = pl.multiple_of(core * SET, ROWS)
            queries[rows, :] = ref[source, pl.ds(start, ROWS), :]
            for kind in range(2):
                at = pl.multiple_of(start + (1 + kind) * ROWS, ROWS)
                pairs[kind, rows, :] = ref[source, pl.ds(at, ROWS), :]

    @pl.when(core == 0)
    def _():
        for ref, zh_from, core_from in (
            (guide_own, zh, 0),
            (guide_core, zh, 1),
            (guide_half, 1 - zh, 0),
            (guide_across, 1 - zh, 1),
        ):
            at = pl.multiple_of(core_from * COLUMN + zh_from * BLOCK, BLOCK)
            queries[pl.ds(pl.multiple_of(TOKENS + at, BLOCK), BLOCK), :] = ref[0]
            pairs[2, pl.ds(at, BLOCK), :] = ref[1]
            pairs[3, pl.ds(at, BLOCK), :] = ref[2]

    @pl.when(core == 1)
    def _():
        for ref, whose in ((got, 1), (sibling, 0)):
            for source in range(Z):
                rows = pl.ds(whose * COLUMN + source * ROWS, ROWS)
                for kind in range(2):
                    start = 2 * SET + kind * ROWS
                    pairs[2 + kind, rows, :] = ref[source, start : start + ROWS, :]
                rows = pl.ds(TOKENS + whose * BLOCK + source * PART, PART)
                queries[rows, :] = ref[source, 2 * SET + 2 * ROWS :, :]
        queries[pl.ds(TOKENS + COLUMN, COLUMN), :] = jnp.zeros((COLUMN, HD), bf16)


def diagonal():
    return lax.broadcasted_iota(jnp.int32, (HD, HD), 0) == lax.broadcasted_iota(
        jnp.int32, (HD, HD), 1
    )


def attend_kernel(queries, *refs):
    pairs, out = refs[:SIDE], refs[SIDE]
    values, scores, weights, stats = refs[SIDE + 1 :]
    for head in range(HEADS):
        for piece in range(SIDE):
            rows = pl.ds(piece * TOKENS, TOKENS)
            values[head, rows, :HD] = pairs[piece][head * 2 + 1]
            values[head, rows, HD:] = jnp.ones((TOKENS, HD), bf16)
    on_diagonal = diagonal()
    parts = [(piece, half) for piece in range(SIDE) for half in range(TOKENS // TILE)]
    tiles = range(HEADS * TOKENS // TILE)
    tops = []
    for tile in tiles:
        head = tile * TILE // TOKENS
        query = queries[tile * TILE : (tile + 1) * TILE, :]
        highest = None
        for index, (piece, half) in enumerate(parts):
            part = lax.dot_general(
                query,
                pairs[piece][head * 2, half * TILE : (half + 1) * TILE, :],
                (((1,), (1,)), ((), ())),
                preferred_element_type=f32,
            )
            scores[tile, :, index * TILE : (index + 1) * TILE] = part
            here = jnp.maximum(part[:, :HD], part[:, HD:])
            highest = here if highest is None else jnp.maximum(highest, here)
        tops.append(jnp.max(highest, axis=1, keepdims=True) * score_scale)
    for tile in tiles:
        for index in range(len(parts)):
            columns = slice(index * TILE, (index + 1) * TILE)
            part = scores[tile, :, columns]
            weights[tile, :, columns] = jnp.exp2(part * score_scale - tops[tile]).astype(bf16)
    for tile in tiles:
        total = jnp.dot(
            weights[tile], values[tile * TILE // TOKENS], preferred_element_type=f32
        )
        weight_sum = total[:, HD:]
        out[tile * TILE : (tile + 1) * TILE, :] = (total[:, :HD] / weight_sum).astype(bf16)
        level = tops[tile] + jnp.log2(weight_sum)
        for part in range(TILE // HD):
            block = level[part * HD : (part + 1) * HD, :]
            row = jnp.sum(jnp.where(on_diagonal, block, 0.0), axis=0, keepdims=True)
            stats[tile * (TILE // HD) + part : tile * (TILE // HD) + part + 1, :] = row
    level = stats[...]
    high = level.astype(bf16).astype(f32)
    middle = (level - high).astype(bf16).astype(f32)
    low = level - high - middle
    block = jnp.concatenate([high, middle, low, jnp.zeros_like(low)], axis=0)
    out[HEADS * TOKENS :, :] = block.astype(bf16)


def terms(value):
    high = value.astype(bf16)
    low = (value - high.astype(f32)).astype(bf16)
    return jnp.concatenate([high, low], axis=0)


def term_dot(value, weight):
    both = jnp.dot(terms(value), weight, preferred_element_type=f32)
    return both[: value.shape[0]] + both[value.shape[0] :]


def prepare_kernel(
    step, place, main_mod, guide_mod, main_head, guide_head, weights, scales, means, shifts
):
    zh, core, zl = place[0], place[1], place[2]
    first = pl.ds(pl.multiple_of((zl * 5 + 2 * zh + core) * HD, HD), HD)
    shared = pl.ds(pl.multiple_of((zl * 5 + 4) * HD, HD), HD)
    guide = pl.ds(pl.multiple_of((zl * 2 + zh) * HD, HD), HD)
    weights[0] = main_head[first, :]
    scales[...] = jnp.zeros_like(scales)
    scales[0:1, :] = 1.0 + main_mod[0, :, first][1:2].astype(f32)

    @pl.when(core == 0)
    def _():
        weights[1] = guide_head[guide, :]
        scales[1:2, :] = 1.0 + guide_mod[0, :, guide][1:2].astype(f32)

    @pl.when(core == 1)
    def _():
        weights[1] = main_head[shared, :]
        scales[1:2, :] = 1.0 + main_mod[0, :, shared][1:2].astype(f32)

    def rows_of(table, order):
        both = table[0].astype(f32)
        shift, scale = both[0:1], 1.0 + both[1:2]
        owner = lax.broadcasted_iota(jnp.int32, scale.shape, 1) >> 7
        rows = [jnp.where(owner == head, scale, 0.0) for head in order] + [shift]
        rows += [jnp.zeros_like(shift)] * (-len(rows) % 8)
        return jnp.concatenate(rows, axis=0)

    main_order = [
        zl * 5 + 2 * zh + core for core in range(CORE) for zh in range(ZH) for zl in range(ZL)
    ] + [zl * 5 + 4 for zl in range(ZL)]
    guide_order = [zl * 2 + zh for zh in range(ZH) for zl in range(ZL)]
    main_rows = term_dot(rows_of(main_mod, main_order), main_head[...])
    guide_rows = term_dot(rows_of(guide_mod, guide_order), guide_head[...])
    main_rows = jnp.concatenate([main_rows, jnp.zeros_like(main_rows)], axis=1)
    guide_rows = jnp.concatenate([jnp.zeros_like(guide_rows), guide_rows], axis=1)
    means[...] = jnp.zeros_like(means)
    for source in range(CORE * Z):
        means[source * 8 : source * 8 + 1, :] = main_rows[source : source + 1]
    for source in range(Z):
        means[source * 8 + 4 : source * 8 + 5, :] = guide_rows[source : source + 1]
        at = (Z + source) * 8 + 4
        means[at : at + 1, :] = main_rows[2 * Z + source % ZL : 2 * Z + source % ZL + 1]
    shifts[...] = jnp.zeros_like(shifts)
    shifts[0:1, :] = main_rows[20:21] + guide_rows[8:9]


def levels_of(part):
    block = part[HEADS * TOKENS :, :].astype(f32)
    return block[0:8] + block[8:16] + block[16:24]


def merge(parts, levels):
    top = levels[0]
    for level in levels[1:]:
        top = jnp.maximum(top, level)
    shares = [jnp.exp2(level - top) for level in levels]
    whole = sum(shares)
    filler = jnp.zeros((HD - 8, HD), f32)
    shares = [jnp.transpose(jnp.concatenate([share / whole, filler], axis=0)) for share in shares]
    tiles = []
    for tile in range(HEADS * TOKENS // HD):
        rows = slice(tile * HD, (tile + 1) * HD)
        tiles.append(
            sum(
                part[rows, :].astype(f32) * share[:, tile : tile + 1]
                for part, share in zip(parts, shares)
            )
        )
    return tiles, top + jnp.log2(whole)


def merge_kernel(*refs):
    parts, result, level = refs[:-2], refs[-2], refs[-1]
    tiles, level[...] = merge(parts, [levels_of(part) for part in parts])
    for tile, value in enumerate(tiles):
        result[tile * HD : (tile + 1) * HD, :] = value


def combine_kernel(place, weights, scales, former, former_level, part, send):
    on_diagonal = diagonal()
    tiles, unused = merge([former, part], [former_level[...], levels_of(part)])
    blocks = TOKENS // HD
    for tile in range(blocks):
        narrow = tiles[blocks + tile // ZH]
        start = tile % ZH * (HD // ZH)
        pieces = []
        for row in range(start, start + HD // ZH, PART):
            pieces += [narrow[row : row + PART]] * ZH
        wide = jnp.concatenate(pieces, axis=0)
        tiles.append(jnp.where(place[1] == 1, wide, tiles[blocks + tile]))
    tiles = tiles[:blocks] + tiles[2 * blocks :]
    flows, stats = [], []
    for head in range(HEADS):
        attended = jnp.concatenate(tiles[head * blocks : (head + 1) * blocks], axis=0).astype(bf16)
        mean = jnp.mean(attended.astype(f32), axis=1, keepdims=True)
        centered = attended.astype(f32) - mean
        square = jnp.sum(centered * centered, axis=1, keepdims=True)
        flow = term_dot(centered * scales[head : head + 1, :], weights[head]).astype(bf16)
        for tile in range(blocks):
            rows = slice(tile * HD, (tile + 1) * HD)
            flows.append(flow[rows])
            both = [
                jnp.sum(jnp.where(on_diagonal, value[rows], 0.0), axis=0, keepdims=True)
                for value in (mean, square)
            ]
            both = jnp.concatenate(both, axis=0)
            high = both.astype(bf16).astype(f32)
            middle = (both - high).astype(bf16).astype(f32)
            stats.append((jnp.concatenate([high, middle], axis=0), both - high - middle))

    gap = jnp.zeros((2, HD), f32)
    for tile in range(blocks):
        other = blocks + tile
        rows = jnp.concatenate([flows[tile], flows[other]], axis=1)
        both = jnp.concatenate(
            [stats[tile][0], stats[other][0], stats[tile][1], gap, stats[other][1], gap],
            axis=0,
        ).astype(bf16)
        for zl in range(ZL):
            send[tile * ZL + zl, 0:ROWS, :] = rows[zl * ROWS : (zl + 1) * ROWS, :]
            send[tile * ZL + zl, ROWS : ROWS + 16, :] = both


def sigma_at(index):
    remaining = 1.0 - index.astype(f32) / STEPS
    return flow_shift * remaining / (1.0 + (flow_shift - 1.0) * remaining)


def final_kernel(step, place, got, means, shifts, latents, velocity, advanced, columns):
    zl = place[2]

    def flows(source):
        return got[source, 0:ROWS, :].astype(f32)

    lower = sum(flows(source) for source in range(Z))
    upper = sum(flows(Z + source) for source in range(Z))
    shared = [sum(flows(Z + zh * ZL + zl) for zl in range(ZL)) for zh in range(ZH)]
    shared = jnp.concatenate([shared[0][:PART], shared[1][PART:]], axis=0)
    upper = upper[:, :C] + shared[:, C:]
    total = lower + jnp.concatenate([upper, jnp.zeros((ROWS, C), f32)], axis=1)

    table = []
    for source in range(CORE * Z):
        block = got[source, ROWS : ROWS + 16, :].astype(f32)
        high = block[:8]
        table.append(high + jnp.concatenate([high[2:], high[:2]], axis=0) + block[8:])
    table = jnp.concatenate(table, axis=0)
    row = lax.broadcasted_iota(jnp.int32, (HD, HD), 0)
    kind, source = row & 7, row >> 3
    token = lax.broadcasted_iota(jnp.int32, (HD, HD), 1)
    second = (source >= Z) & (((source - Z) >> 2) == ((token >> 4) & 1))

    def gathered(count, of_mean, of_square):
        mean = jnp.sum(jnp.where(of_mean, table, 0.0), axis=0, keepdims=True) / count
        apart = jnp.where(of_mean, table - mean, 0.0)
        spread = jnp.where(of_square, table, 0.0) + HD * (apart * apart)
        spread = jnp.sum(spread, axis=0, keepdims=True) / (count * HD)
        return apart, lax.rsqrt(spread + epsilon)

    main, main_shrink = gathered(
        20, (kind == 0) | ((kind == 4) & second), (kind == 1) | ((kind == 5) & second)
    )
    guide, guide_shrink = gathered(8, (kind == 4) & (source < Z), (kind == 5) & (source < Z))
    block = main + guide
    block = jnp.where(row == 2, main_shrink, jnp.where(row == 3, guide_shrink, block))
    columns[...] = jnp.transpose(block)
    mine = columns[pl.ds(pl.multiple_of(zl * ROWS, ROWS), ROWS), :]
    lane = lax.broadcasted_iota(jnp.int32, (ROWS, HD), 1)
    shrink = jnp.where(lane < C, mine[:, 2:3], mine[:, 3:4])
    high = means[...].astype(bf16)
    moved = term_dot(mine, high) + jnp.dot(
        mine.astype(bf16), (means[...] - high.astype(f32)).astype(bf16), preferred_element_type=f32
    )
    flow = shrink * (total + moved) + shifts[0:1, :]
    main_flow, guide_flow = flow[:, :C], flow[:, C:]
    result = guide_flow + guidance * (main_flow - guide_flow)
    now = jnp.full((1, 1), step[0], jnp.int32)
    velocity[0] = result
    advanced[0] = latents[0] + (sigma_at(now + 1) - sigma_at(now)) * result


def plane_shift(array, by, axis_of_core):
    pairs = []
    for x in range(X):
        for y in range(Y):
            for core in range(CORE):
                if axis_of_core[core] == "x":
                    to = ((x + by) % X, y)
                else:
                    to = (x, (y + by) % Y)
                pairs.append(((x * Y + y) * CORE + core, (to[0] * Y + to[1]) * CORE + core))
    return lax.ppermute(array, ("x", "y", "core"), pairs)


SHIFTS = (-1, 1, 2)


def attend(queries, pairs):
    rows, tiles = HEADS * TOKENS, HEADS * TOKENS // TILE
    return pl.pallas_call(
        attend_kernel,
        out_shape=shape(rows + STAT, HD),
        in_specs=[VMEM] * (1 + SIDE),
        out_specs=VMEM,
        scratch_shapes=[
            pltpu.VMEM((HEADS, KEYS, 2 * HD), bf16),
            pltpu.VMEM((tiles, TILE, KEYS), f32),
            pltpu.VMEM((tiles, TILE, KEYS), bf16),
            pltpu.VMEM((8, HD), f32),
        ],
        compiler_params=params(32),
        cost_estimate=pl.CostEstimate(
            flops=4 * rows * KEYS * HD,
            bytes_accessed=4 * HEADS * KEYS * HD,
            transcendentals=rows * KEYS,
        ),
        name="attend",
    )(queries, *pairs)


def on_device(
    main_query,
    main_key,
    main_value,
    guide_query,
    guide_key,
    guide_value,
    latents,
    step_index,
    main_mod,
    guide_mod,
    main_head,
    guide_head,
):
    place = jnp.stack([lax.axis_index(name) for name in ("zh", "core", "zl")]).astype(jnp.int32)
    guide_send, guide_own = pl.pallas_call(
        pack_guide_kernel,
        out_shape=(shape(3, BLOCK, HD),) * 2,
        in_specs=[SMEM] + [ANY] * 3,
        out_specs=(VMEM,) * 2,
        scratch_shapes=[pltpu.SemaphoreType.DMA((6,))],
        compiler_params=params(16),
        name="pack_guide",
    )(place, guide_query, guide_key, guide_value)
    send = pl.pallas_call(
        pack_kernel,
        out_shape=shape(Z, MESSAGE, HD),
        in_specs=[ANY] * 3,
        out_specs=VMEM,
        scratch_shapes=[
            pltpu.VMEM((3, ROWS, 20 * HD), bf16),
            pltpu.SemaphoreType.DMA((3,)),
        ],
        compiler_params=params(60),
        name="pack",
    )(main_query, main_key, main_value)
    whole = lambda *dims: pl.BlockSpec(dims, lambda i, step, place: (0,) * len(dims))
    row = lambda *dims: pl.BlockSpec(dims, lambda i, step, place: (step[0], 0, 0))
    weights, scales, means, shifts = pl.pallas_call(
        prepare_kernel,
        out_shape=(
            shape(HEADS, HD, C),
            shape(8, HD, dtype=f32),
            shape(HD, HD, dtype=f32),
            shape(8, HD, dtype=f32),
        ),
        grid_spec=pltpu.PrefetchScalarGridSpec(
            num_scalar_prefetch=2,
            grid=(1,),
            in_specs=[
                row(1, 2, 20 * HD),
                row(1, 2, 8 * HD),
                whole(20 * HD, C),
                whole(8 * HD, C),
            ],
            out_specs=[whole(HEADS, HD, C), whole(8, HD), whole(HD, HD), whole(8, HD)],
        ),
        compiler_params=params(16),
        name="prepare",
    )(step_index, place, main_mod, guide_mod, main_head, guide_head)
    halves = ("zh", "core")
    guide_core = lax.ppermute(guide_own, halves, [(1, 0), (3, 2)])
    guide_half = lax.ppermute(guide_send, halves, [(0, 2), (2, 0)])
    guide_across = lax.ppermute(guide_send, halves, [(1, 2), (3, 0)])
    got = lax.all_to_all(send, ("zh", "zl"), split_axis=0, concat_axis=0, tiled=True)
    got, guide_core, guide_half, guide_across, weights, scales, means, shifts = (
        lax.optimization_barrier(
            (got, guide_core, guide_half, guide_across, weights, scales, means, shifts)
        )
    )
    sibling = lax.ppermute(got, "core", [(0, 1), (1, 0)])
    queries, pairs = pl.pallas_call(
        unpack_kernel,
        out_shape=(shape(HEADS * TOKENS, HD), shape(2 * HEADS, TOKENS, HD)),
        in_specs=[SMEM] + [VMEM] * 6,
        out_specs=(VMEM,) * 2,
        compiler_params=params(16),
        name="unpack",
    )(place, got, sibling, guide_own, guide_core, guide_half, guide_across)
    all_queries = [queries] + [plane_shift(queries, by, "xy") for by in SHIFTS]
    all_pairs = [pairs] + [plane_shift(pairs, by, "yx") for by in SHIFTS]
    parts = [attend(q, all_pairs) for q in all_queries]
    parts[1:] = [plane_shift(p, -by, "xy") for p, by in zip(parts[1:], SHIFTS)]
    former, level = pl.pallas_call(
        merge_kernel,
        out_shape=(shape(HEADS * TOKENS, HD, dtype=f32), shape(8, HD, dtype=f32)),
        in_specs=[VMEM] * (SIDE - 1),
        out_specs=(VMEM,) * 2,
        compiler_params=params(16),
        name="merge",
    )(*parts[:-1])
    send = pl.pallas_call(
        combine_kernel,
        out_shape=shape(CORE * Z, ROWS + 16, HD),
        in_specs=[SMEM] + [VMEM] * 5,
        out_specs=VMEM,
        compiler_params=params(16),
        name="combine",
    )(place, weights, scales, former, level, parts[-1])
    got = lax.all_to_all(send, ("core", "zh", "zl"), split_axis=0, concat_axis=0, tiled=True)
    velocity, advanced = pl.pallas_call(
        final_kernel,
        out_shape=(shape(1, ROWS, C, dtype=f32),) * 2,
        in_specs=[SMEM] * 2 + [VMEM] * 4,
        out_specs=(VMEM,) * 2,
        scratch_shapes=[pltpu.VMEM((HD, HD), f32)],
        compiler_params=params(16),
        name="final",
    )(step_index, place, got, means, shifts, latents)
    return velocity, advanced


def solution(mesh):
    fine = Mesh(mesh.devices.reshape(ZL, X, Y, ZH, CORE), ("zl", "x", "y", "zh", "core"))
    seq = ("x", "y", "zh", "core")
    return jax.shard_map(
        on_device,
        mesh=fine,
        in_specs=(P(seq, "zl", None),) * 3
        + (P(seq, None, "zl"),) * 3
        + (P(seq, "zl", None),)
        + (P(),) * 5,
        out_specs=(P(seq, "zl", None),) * 2,
        check_vma=False,
    )
```

```python
import math

import jax
import jax.numpy as jnp
from jax import lax
from jax.experimental import pallas as pl
from jax.experimental.pallas import tpu as pltpu
from jax.sharding import Mesh, PartitionSpec as P

HD = 128
C = 64
STEPS = 50
ZL, X, Y, ZH, CORE = 4, 4, 4, 2, 2
Z = ZL * ZH
SIDE = 4
ROWS = 32
PART = ROWS // ZH
SET = 3 * ROWS
MESSAGE = 2 * SET + 2 * ROWS + PART
BLOCK = 128
COLUMN = ROWS * Z
TOKENS = COLUMN * CORE
TILE = 256
HEADS = 2
STAT = 32
KEYS = SIDE * TOKENS

guidance = 2.5
flow_shift = 3.0
epsilon = 1e-06
score_scale = math.log2(math.e) / math.sqrt(HD)

f32 = jnp.float32
bf16 = jnp.bfloat16
VMEM = pl.BlockSpec(memory_space=pltpu.VMEM)
SMEM = pl.BlockSpec(memory_space=pltpu.SMEM)
ANY = pl.BlockSpec(memory_space=pl.ANY)


def shape(*dims, dtype=bf16):
    return jax.ShapeDtypeStruct(dims, dtype)


def params(mib):
    return pltpu.CompilerParams(vmem_limit_bytes=mib * 1024 * 1024)


def pack_guide_kernel(place, gq, gk, gv, send, own, sems):
    copies = []
    for head, to in ((1 - place[0], send), (place[0], own)):
        lanes = pl.ds(pl.multiple_of(head * HD, HD), HD)
        for kind, ref in enumerate((gq, gk, gv)):
            copy = pltpu.make_async_copy(ref.at[0, :, lanes], to.at[kind], sems.at[len(copies)])
            copy.start()
            copies.append(copy)
    for copy in copies:
        copy.wait()


def pack_kernel(mq, mk, mv, send, main, sems):
    copies = []
    for kind, ref in enumerate((mq, mk, mv)):
        copy = pltpu.make_async_copy(ref.at[0], main.at[kind], sems.at[kind])
        copy.start()
        copies.append(copy)
    for kind, copy in enumerate(copies):
        copy.wait()
        for zh_to in range(ZH):
            for zl_to in range(ZL):
                to = zh_to * ZL + zl_to
                for slot in range(2):
                    head = zl_to * 5 + 2 * zh_to + slot
                    start = slot * SET + kind * ROWS
                    send[to, start : start + ROWS, :] = main[kind, :, head * HD : (head + 1) * HD]
                lanes = slice((zl_to * 5 + 4) * HD, (zl_to * 5 + 5) * HD)
                if kind == 0:
                    rows = slice(zh_to * PART, (zh_to + 1) * PART)
                    send[to, 2 * SET + 2 * ROWS :, :] = main[0, rows, lanes]
                else:
                    start = 2 * SET + (kind - 1) * ROWS
                    send[to, start : start + ROWS, :] = main[kind, :, lanes]


def unpack_kernel(
    place, got, sibling, guide_own, guide_core, guide_half, guide_across, queries, pairs
):
    zh, core = place[0], place[1]
    for ref, whose in ((got, core), (sibling, 1 - core)):
        base = whose * COLUMN
        for source in range(Z):
            rows = pl.ds(pl.multiple_of(base + source * ROWS, ROWS), ROWS)
            start = pl.multiple_of(core * SET, ROWS)
            queries[rows, :] = ref[source, pl.ds(start, ROWS), :]
            for kind in range(2):
                at = pl.multiple_of(start + (1 + kind) * ROWS, ROWS)
                pairs[kind, rows, :] = ref[source, pl.ds(at, ROWS), :]

    @pl.when(core == 0)
    def _():
        for ref, zh_from, core_from in (
            (guide_own, zh, 0),
            (guide_core, zh, 1),
            (guide_half, 1 - zh, 0),
            (guide_across, 1 - zh, 1),
        ):
            at = pl.multiple_of(core_from * COLUMN + zh_from * BLOCK, BLOCK)
            queries[pl.ds(pl.multiple_of(TOKENS + at, BLOCK), BLOCK), :] = ref[0]
            pairs[2, pl.ds(at, BLOCK), :] = ref[1]
            pairs[3, pl.ds(at, BLOCK), :] = ref[2]

    @pl.when(core == 1)
    def _():
        for ref, whose in ((got, 1), (sibling, 0)):
            for source in range(Z):
                rows = pl.ds(whose * COLUMN + source * ROWS, ROWS)
                for kind in range(2):
                    start = 2 * SET + kind * ROWS
                    pairs[2 + kind, rows, :] = ref[source, start : start + ROWS, :]
                rows = pl.ds(TOKENS + whose * BLOCK + source * PART, PART)
                queries[rows, :] = ref[source, 2 * SET + 2 * ROWS :, :]
        queries[pl.ds(TOKENS + COLUMN, COLUMN), :] = jnp.zeros((COLUMN, HD), bf16)


def diagonal():
    return lax.broadcasted_iota(jnp.int32, (HD, HD), 0) == lax.broadcasted_iota(
        jnp.int32, (HD, HD), 1
    )


def attend_kernel(queries, *refs):
    pairs, out = refs[:SIDE], refs[SIDE]
    values, scores, weights, stats = refs[SIDE + 1 :]
    for head in range(HEADS):
        for piece in range(SIDE):
            rows = pl.ds(piece * TOKENS, TOKENS)
            values[head, rows, :HD] = pairs[piece][head * 2 + 1]
            values[head, rows, HD:] = jnp.ones((TOKENS, HD), bf16)
    on_diagonal = diagonal()
    parts = [(piece, half) for piece in range(SIDE) for half in range(TOKENS // TILE)]
    tiles = range(HEADS * TOKENS // TILE)
    tops = []
    for tile in tiles:
        head = tile * TILE // TOKENS
        query = queries[tile * TILE : (tile + 1) * TILE, :]
        highest = None
        for index, (piece, half) in enumerate(parts):
            part = lax.dot_general(
                query,
                pairs[piece][head * 2, half * TILE : (half + 1) * TILE, :],
                (((1,), (1,)), ((), ())),
                preferred_element_type=f32,
            )
            scores[tile, :, index * TILE : (index + 1) * TILE] = part
            here = jnp.maximum(part[:, :HD], part[:, HD:])
            highest = here if highest is None else jnp.maximum(highest, here)
        tops.append(jnp.max(highest, axis=1, keepdims=True) * score_scale)
    for tile in tiles:
        for index in range(len(parts)):
            columns = slice(index * TILE, (index + 1) * TILE)
            part = scores[tile, :, columns]
            weights[tile, :, columns] = jnp.exp2(part * score_scale - tops[tile]).astype(bf16)
    for tile in tiles:
        total = jnp.dot(
            weights[tile], values[tile * TILE // TOKENS], preferred_element_type=f32
        )
        weight_sum = total[:, HD:]
        out[tile * TILE : (tile + 1) * TILE, :] = (total[:, :HD] / weight_sum).astype(bf16)
        level = tops[tile] + jnp.log2(weight_sum)
        for part in range(TILE // HD):
            block = level[part * HD : (part + 1) * HD, :]
            row = jnp.sum(jnp.where(on_diagonal, block, 0.0), axis=0, keepdims=True)
            stats[tile * (TILE // HD) + part : tile * (TILE // HD) + part + 1, :] = row
    level = stats[...]
    high = level.astype(bf16).astype(f32)
    middle = (level - high).astype(bf16).astype(f32)
    low = level - high - middle
    block = jnp.concatenate([high, middle, low, jnp.zeros_like(low)], axis=0)
    out[HEADS * TOKENS :, :] = block.astype(bf16)


def terms(value):
    high = value.astype(bf16)
    low = (value - high.astype(f32)).astype(bf16)
    return jnp.concatenate([high, low], axis=0)


def term_dot(value, weight):
    both = jnp.dot(terms(value), weight, preferred_element_type=f32)
    return both[: value.shape[0]] + both[value.shape[0] :]


def prepare_kernel(
    step, place, main_mod, guide_mod, main_head, guide_head, weights, scales, means, shifts
):
    zh, core, zl = place[0], place[1], place[2]
    first = pl.ds(pl.multiple_of((zl * 5 + 2 * zh + core) * HD, HD), HD)
    shared = pl.ds(pl.multiple_of((zl * 5 + 4) * HD, HD), HD)
    guide = pl.ds(pl.multiple_of((zl * 2 + zh) * HD, HD), HD)
    weights[0] = main_head[first, :]
    scales[...] = jnp.zeros_like(scales)
    scales[0:1, :] = 1.0 + main_mod[0, :, first][1:2].astype(f32)

    @pl.when(core == 0)
    def _():
        weights[1] = guide_head[guide, :]
        scales[1:2, :] = 1.0 + guide_mod[0, :, guide][1:2].astype(f32)

    @pl.when(core == 1)
    def _():
        weights[1] = main_head[shared, :]
        scales[1:2, :] = 1.0 + main_mod[0, :, shared][1:2].astype(f32)

    def rows_of(table, order):
        both = table[0].astype(f32)
        shift, scale = both[0:1], 1.0 + both[1:2]
        owner = lax.broadcasted_iota(jnp.int32, scale.shape, 1) >> 7
        rows = [jnp.where(owner == head, scale, 0.0) for head in order] + [shift]
        rows += [jnp.zeros_like(shift)] * (-len(rows) % 8)
        return jnp.concatenate(rows, axis=0)

    main_order = [
        zl * 5 + 2 * zh + core for core in range(CORE) for zh in range(ZH) for zl in range(ZL)
    ] + [zl * 5 + 4 for zl in range(ZL)]
    guide_order = [zl * 2 + zh for zh in range(ZH) for zl in range(ZL)]
    main_rows = term_dot(rows_of(main_mod, main_order), main_head[...])
    guide_rows = term_dot(rows_of(guide_mod, guide_order), guide_head[...])
    main_rows = jnp.concatenate([main_rows, jnp.zeros_like(main_rows)], axis=1)
    guide_rows = jnp.concatenate([jnp.zeros_like(guide_rows), guide_rows], axis=1)
    means[...] = jnp.zeros_like(means)
    for source in range(CORE * Z):
        means[source * 8 : source * 8 + 1, :] = main_rows[source : source + 1]
    for source in range(Z):
        means[source * 8 + 4 : source * 8 + 5, :] = guide_rows[source : source + 1]
        at = (Z + source) * 8 + 4
        means[at : at + 1, :] = main_rows[2 * Z + source % ZL : 2 * Z + source % ZL + 1]
    shifts[...] = jnp.zeros_like(shifts)
    shifts[0:1, :] = main_rows[20:21] + guide_rows[8:9]


def levels_of(part):
    block = part[HEADS * TOKENS :, :].astype(f32)
    return block[0:8] + block[8:16] + block[16:24]


def merge(parts, levels):
    top = levels[0]
    for level in levels[1:]:
        top = jnp.maximum(top, level)
    shares = [jnp.exp2(level - top) for level in levels]
    whole = sum(shares)
    filler = jnp.zeros((HD - 8, HD), f32)
    shares = [jnp.transpose(jnp.concatenate([share / whole, filler], axis=0)) for share in shares]
    tiles = []
    for tile in range(HEADS * TOKENS // HD):
        rows = slice(tile * HD, (tile + 1) * HD)
        tiles.append(
            sum(
                part[rows, :].astype(f32) * share[:, tile : tile + 1]
                for part, share in zip(parts, shares)
            )
        )
    return tiles, top + jnp.log2(whole)


def merge_kernel(*refs):
    parts, result, level = refs[:-2], refs[-2], refs[-1]
    tiles, level[...] = merge(parts, [levels_of(part) for part in parts])
    for tile, value in enumerate(tiles):
        result[tile * HD : (tile + 1) * HD, :] = value


def combine_kernel(place, weights, scales, former, former_level, part, send):
    on_diagonal = diagonal()
    tiles, unused = merge([former, part], [former_level[...], levels_of(part)])
    blocks = TOKENS // HD
    for tile in range(blocks):
        narrow = tiles[blocks + tile // ZH]
        start = tile % ZH * (HD // ZH)
        pieces = []
        for row in range(start, start + HD // ZH, PART):
            pieces += [narrow[row : row + PART]] * ZH
        wide = jnp.concatenate(pieces, axis=0)
        tiles.append(jnp.where(place[1] == 1, wide, tiles[blocks + tile]))
    tiles = tiles[:blocks] + tiles[2 * blocks :]
    flows, stats = [], []
    for head in range(HEADS):
        attended = jnp.concatenate(tiles[head * blocks : (head + 1) * blocks], axis=0).astype(bf16)
        mean = jnp.mean(attended.astype(f32), axis=1, keepdims=True)
        centered = attended.astype(f32) - mean
        square = jnp.sum(centered * centered, axis=1, keepdims=True)
        scaled = (centered * scales[head : head + 1, :]).astype(bf16)
        flow = jnp.dot(scaled, weights[head], preferred_element_type=f32).astype(bf16)
        for tile in range(blocks):
            rows = slice(tile * HD, (tile + 1) * HD)
            flows.append(flow[rows])
            both = [
                jnp.sum(jnp.where(on_diagonal, value[rows], 0.0), axis=0, keepdims=True)
                for value in (mean, square)
            ]
            both = jnp.concatenate(both, axis=0)
            high = both.astype(bf16).astype(f32)
            middle = (both - high).astype(bf16).astype(f32)
            stats.append((jnp.concatenate([high, middle], axis=0), both - high - middle))

    gap = jnp.zeros((2, HD), f32)
    for tile in range(blocks):
        other = blocks + tile
        rows = jnp.concatenate([flows[tile], flows[other]], axis=1)
        both = jnp.concatenate(
            [stats[tile][0], stats[other][0], stats[tile][1], gap, stats[other][1], gap],
            axis=0,
        ).astype(bf16)
        for zl in range(ZL):
            send[tile * ZL + zl, 0:ROWS, :] = rows[zl * ROWS : (zl + 1) * ROWS, :]
            send[tile * ZL + zl, ROWS : ROWS + 16, :] = both


def sigma_at(index):
    remaining = 1.0 - index.astype(f32) / STEPS
    return flow_shift * remaining / (1.0 + (flow_shift - 1.0) * remaining)


def final_kernel(step, place, got, means, shifts, latents, velocity, advanced, columns):
    zl = place[2]

    def flows(source):
        return got[source, 0:ROWS, :].astype(f32)

    lower = sum(flows(source) for source in range(Z))
    upper = sum(flows(Z + source) for source in range(Z))
    shared = [sum(flows(Z + zh * ZL + zl) for zl in range(ZL)) for zh in range(ZH)]
    shared = jnp.concatenate([shared[0][:PART], shared[1][PART:]], axis=0)
    upper = upper[:, :C] + shared[:, C:]
    total = lower + jnp.concatenate([upper, jnp.zeros((ROWS, C), f32)], axis=1)

    table = []
    for source in range(CORE * Z):
        block = got[source, ROWS : ROWS + 16, :].astype(f32)
        high = block[:8]
        table.append(high + jnp.concatenate([high[2:], high[:2]], axis=0) + block[8:])
    table = jnp.concatenate(table, axis=0)
    row = lax.broadcasted_iota(jnp.int32, (HD, HD), 0)
    kind, source = row & 7, row >> 3
    token = lax.broadcasted_iota(jnp.int32, (HD, HD), 1)
    second = (source >= Z) & (((source - Z) >> 2) == ((token >> 4) & 1))

    def gathered(count, of_mean, of_square):
        mean = jnp.sum(jnp.where(of_mean, table, 0.0), axis=0, keepdims=True) / count
        apart = jnp.where(of_mean, table - mean, 0.0)
        spread = jnp.where(of_square, table, 0.0) + HD * (apart * apart)
        spread = jnp.sum(spread, axis=0, keepdims=True) / (count * HD)
        return apart, lax.rsqrt(spread + epsilon)

    main, main_shrink = gathered(
        20, (kind == 0) | ((kind == 4) & second), (kind == 1) | ((kind == 5) & second)
    )
    guide, guide_shrink = gathered(8, (kind == 4) & (source < Z), (kind == 5) & (source < Z))
    block = main + guide
    block = jnp.where(row == 2, main_shrink, jnp.where(row == 3, guide_shrink, block))
    columns[...] = jnp.transpose(block)
    mine = columns[pl.ds(pl.multiple_of(zl * ROWS, ROWS), ROWS), :]
    lane = lax.broadcasted_iota(jnp.int32, (ROWS, HD), 1)
    shrink = jnp.where(lane < C, mine[:, 2:3], mine[:, 3:4])
    high = means[...].astype(bf16)
    moved = term_dot(mine, high) + jnp.dot(
        mine.astype(bf16), (means[...] - high.astype(f32)).astype(bf16), preferred_element_type=f32
    )
    flow = shrink * (total + moved) + shifts[0:1, :]
    main_flow, guide_flow = flow[:, :C], flow[:, C:]
    result = guide_flow + guidance * (main_flow - guide_flow)
    now = jnp.full((1, 1), step[0], jnp.int32)
    velocity[0] = result
    advanced[0] = latents[0] + (sigma_at(now + 1) - sigma_at(now)) * result


def plane_shift(array, by, axis_of_core):
    pairs = []
    for x in range(X):
        for y in range(Y):
            for core in range(CORE):
                if axis_of_core[core] == "x":
                    to = ((x + by) % X, y)
                else:
                    to = (x, (y + by) % Y)
                pairs.append(((x * Y + y) * CORE + core, (to[0] * Y + to[1]) * CORE + core))
    return lax.ppermute(array, ("x", "y", "core"), pairs)


SHIFTS = (-1, 1, 2)


def attend(queries, pairs):
    rows, tiles = HEADS * TOKENS, HEADS * TOKENS // TILE
    return pl.pallas_call(
        attend_kernel,
        out_shape=shape(rows + STAT, HD),
        in_specs=[VMEM] * (1 + SIDE),
        out_specs=VMEM,
        scratch_shapes=[
            pltpu.VMEM((HEADS, KEYS, 2 * HD), bf16),
            pltpu.VMEM((tiles, TILE, KEYS), f32),
            pltpu.VMEM((tiles, TILE, KEYS), bf16),
            pltpu.VMEM((8, HD), f32),
        ],
        compiler_params=params(32),
        cost_estimate=pl.CostEstimate(
            flops=4 * rows * KEYS * HD,
            bytes_accessed=4 * HEADS * KEYS * HD,
            transcendentals=rows * KEYS,
        ),
        name="attend",
    )(queries, *pairs)


def on_device(
    main_query,
    main_key,
    main_value,
    guide_query,
    guide_key,
    guide_value,
    latents,
    step_index,
    main_mod,
    guide_mod,
    main_head,
    guide_head,
):
    place = jnp.stack([lax.axis_index(name) for name in ("zh", "core", "zl")]).astype(jnp.int32)
    guide_send, guide_own = pl.pallas_call(
        pack_guide_kernel,
        out_shape=(shape(3, BLOCK, HD),) * 2,
        in_specs=[SMEM] + [ANY] * 3,
        out_specs=(VMEM,) * 2,
        scratch_shapes=[pltpu.SemaphoreType.DMA((6,))],
        compiler_params=params(16),
        name="pack_guide",
    )(place, guide_query, guide_key, guide_value)
    send = pl.pallas_call(
        pack_kernel,
        out_shape=shape(Z, MESSAGE, HD),
        in_specs=[ANY] * 3,
        out_specs=VMEM,
        scratch_shapes=[
            pltpu.VMEM((3, ROWS, 20 * HD), bf16),
            pltpu.SemaphoreType.DMA((3,)),
        ],
        compiler_params=params(60),
        name="pack",
    )(main_query, main_key, main_value)
    whole = lambda *dims: pl.BlockSpec(dims, lambda i, step, place: (0,) * len(dims))
    row = lambda *dims: pl.BlockSpec(dims, lambda i, step, place: (step[0], 0, 0))
    weights, scales, means, shifts = pl.pallas_call(
        prepare_kernel,
        out_shape=(
            shape(HEADS, HD, C),
            shape(8, HD, dtype=f32),
            shape(HD, HD, dtype=f32),
            shape(8, HD, dtype=f32),
        ),
        grid_spec=pltpu.PrefetchScalarGridSpec(
            num_scalar_prefetch=2,
            grid=(1,),
            in_specs=[
                row(1, 2, 20 * HD),
                row(1, 2, 8 * HD),
                whole(20 * HD, C),
                whole(8 * HD, C),
            ],
            out_specs=[whole(HEADS, HD, C), whole(8, HD), whole(HD, HD), whole(8, HD)],
        ),
        compiler_params=params(16),
        name="prepare",
    )(step_index, place, main_mod, guide_mod, main_head, guide_head)
    halves = ("zh", "core")
    guide_core = lax.ppermute(guide_own, halves, [(1, 0), (3, 2)])
    guide_half = lax.ppermute(guide_send, halves, [(0, 2), (2, 0)])
    guide_across = lax.ppermute(guide_send, halves, [(1, 2), (3, 0)])
    got = lax.all_to_all(send, ("zh", "zl"), split_axis=0, concat_axis=0, tiled=True)
    got, guide_core, guide_half, guide_across, weights, scales, means, shifts = (
        lax.optimization_barrier(
            (got, guide_core, guide_half, guide_across, weights, scales, means, shifts)
        )
    )
    sibling = lax.ppermute(got, "core", [(0, 1), (1, 0)])
    queries, pairs = pl.pallas_call(
        unpack_kernel,
        out_shape=(shape(HEADS * TOKENS, HD), shape(2 * HEADS, TOKENS, HD)),
        in_specs=[SMEM] + [VMEM] * 6,
        out_specs=(VMEM,) * 2,
        compiler_params=params(16),
        name="unpack",
    )(place, got, sibling, guide_own, guide_core, guide_half, guide_across)
    all_queries = [queries] + [plane_shift(queries, by, "xy") for by in SHIFTS]
    all_pairs = [pairs] + [plane_shift(pairs, by, "yx") for by in SHIFTS]
    parts = [attend(q, all_pairs) for q in all_queries]
    parts[1:] = [plane_shift(p, -by, "xy") for p, by in zip(parts[1:], SHIFTS)]
    former, level = pl.pallas_call(
        merge_kernel,
        out_shape=(shape(HEADS * TOKENS, HD, dtype=f32), shape(8, HD, dtype=f32)),
        in_specs=[VMEM] * (SIDE - 1),
        out_specs=(VMEM,) * 2,
        compiler_params=params(16),
        name="merge",
    )(*parts[:-1])
    send = pl.pallas_call(
        combine_kernel,
        out_shape=shape(CORE * Z, ROWS + 16, HD),
        in_specs=[SMEM] + [VMEM] * 5,
        out_specs=VMEM,
        compiler_params=params(16),
        name="combine",
    )(place, weights, scales, former, level, parts[-1])
    got = lax.all_to_all(send, ("core", "zh", "zl"), split_axis=0, concat_axis=0, tiled=True)
    velocity, advanced = pl.pallas_call(
        final_kernel,
        out_shape=(shape(1, ROWS, C, dtype=f32),) * 2,
        in_specs=[SMEM] * 2 + [VMEM] * 4,
        out_specs=(VMEM,) * 2,
        scratch_shapes=[pltpu.VMEM((HD, HD), f32)],
        compiler_params=params(16),
        name="final",
    )(step_index, place, got, means, shifts, latents)
    return velocity, advanced


def solution(mesh):
    fine = Mesh(mesh.devices.reshape(ZL, X, Y, ZH, CORE), ("zl", "x", "y", "zh", "core"))
    seq = ("x", "y", "zh", "core")
    return jax.shard_map(
        on_device,
        mesh=fine,
        in_specs=(P(seq, "zl", None),) * 3
        + (P(seq, None, "zl"),) * 3
        + (P(seq, "zl", None),)
        + (P(),) * 5,
        out_specs=(P(seq, "zl", None),) * 2,
        check_vma=False,
    )
```

```python
import math

import jax
import jax.numpy as jnp
from jax import lax
from jax.experimental import pallas as pl
from jax.experimental.pallas import tpu as pltpu
from jax.sharding import Mesh, PartitionSpec as P

HD = 128
C = 64
STEPS = 50
ZL, X, Y, ZH, CORE = 4, 4, 4, 2, 2
Z = ZL * ZH
SIDE = 4
ROWS = 32
PART = ROWS // ZH
SET = 3 * ROWS
MESSAGE = 2 * SET + 2 * ROWS + PART
BLOCK = 128
COLUMN = ROWS * Z
TOKENS = COLUMN * CORE
TILE = 256
HEADS = 2
STAT = 32
KEYS = SIDE * TOKENS

guidance = 2.5
flow_shift = 3.0
epsilon = 1e-06
score_scale = math.log2(math.e) / math.sqrt(HD)

f32 = jnp.float32
bf16 = jnp.bfloat16
VMEM = pl.BlockSpec(memory_space=pltpu.VMEM)
SMEM = pl.BlockSpec(memory_space=pltpu.SMEM)
ANY = pl.BlockSpec(memory_space=pl.ANY)


def shape(*dims, dtype=bf16):
    return jax.ShapeDtypeStruct(dims, dtype)


def params(mib):
    return pltpu.CompilerParams(vmem_limit_bytes=mib * 1024 * 1024)


def pack_guide_kernel(place, gq, gk, gv, send, own, sems):
    copies = []
    for head, to in ((1 - place[0], send), (place[0], own)):
        lanes = pl.ds(pl.multiple_of(head * HD, HD), HD)
        for kind, ref in enumerate((gq, gk, gv)):
            copy = pltpu.make_async_copy(ref.at[0, :, lanes], to.at[kind], sems.at[len(copies)])
            copy.start()
            copies.append(copy)
    for copy in copies:
        copy.wait()


def pack_kernel(mq, mk, mv, send, main, sems):
    copies = []
    for kind, ref in enumerate((mq, mk, mv)):
        copy = pltpu.make_async_copy(ref.at[0], main.at[kind], sems.at[kind])
        copy.start()
        copies.append(copy)
    for kind, copy in enumerate(copies):
        copy.wait()
        for zh_to in range(ZH):
            for zl_to in range(ZL):
                to = zh_to * ZL + zl_to
                for slot in range(2):
                    head = zl_to * 5 + 2 * zh_to + slot
                    start = slot * SET + kind * ROWS
                    send[to, start : start + ROWS, :] = main[kind, :, head * HD : (head + 1) * HD]
                lanes = slice((zl_to * 5 + 4) * HD, (zl_to * 5 + 5) * HD)
                if kind == 0:
                    rows = slice(zh_to * PART, (zh_to + 1) * PART)
                    send[to, 2 * SET + 2 * ROWS :, :] = main[0, rows, lanes]
                else:
                    start = 2 * SET + (kind - 1) * ROWS
                    send[to, start : start + ROWS, :] = main[kind, :, lanes]


def unpack_kernel(
    place, got, sibling, guide_own, guide_core, guide_half, guide_across, queries, pairs
):
    zh, core = place[0], place[1]
    for ref, whose in ((got, core), (sibling, 1 - core)):
        base = whose * COLUMN
        for source in range(Z):
            rows = pl.ds(pl.multiple_of(base + source * ROWS, ROWS), ROWS)
            start = pl.multiple_of(core * SET, ROWS)
            queries[rows, :] = ref[source, pl.ds(start, ROWS), :]
            for kind in range(2):
                at = pl.multiple_of(start + (1 + kind) * ROWS, ROWS)
                pairs[kind, rows, :] = ref[source, pl.ds(at, ROWS), :]

    @pl.when(core == 0)
    def _():
        for ref, zh_from, core_from in (
            (guide_own, zh, 0),
            (guide_core, zh, 1),
            (guide_half, 1 - zh, 0),
            (guide_across, 1 - zh, 1),
        ):
            at = pl.multiple_of(core_from * COLUMN + zh_from * BLOCK, BLOCK)
            queries[pl.ds(pl.multiple_of(TOKENS + at, BLOCK), BLOCK), :] = ref[0]
            pairs[2, pl.ds(at, BLOCK), :] = ref[1]
            pairs[3, pl.ds(at, BLOCK), :] = ref[2]

    @pl.when(core == 1)
    def _():
        for ref, whose in ((got, 1), (sibling, 0)):
            for source in range(Z):
                rows = pl.ds(whose * COLUMN + source * ROWS, ROWS)
                for kind in range(2):
                    start = 2 * SET + kind * ROWS
                    pairs[2 + kind, rows, :] = ref[source, start : start + ROWS, :]
                rows = pl.ds(TOKENS + whose * BLOCK + source * PART, PART)
                queries[rows, :] = ref[source, 2 * SET + 2 * ROWS :, :]
        queries[pl.ds(TOKENS + COLUMN, COLUMN), :] = jnp.zeros((COLUMN, HD), bf16)


def diagonal():
    return lax.broadcasted_iota(jnp.int32, (HD, HD), 0) == lax.broadcasted_iota(
        jnp.int32, (HD, HD), 1
    )


def attend_kernel(queries, *refs):
    pairs, out = refs[:SIDE], refs[SIDE]
    values, scores, weights, stats = refs[SIDE + 1 :]
    for head in range(HEADS):
        for piece in range(SIDE):
            rows = pl.ds(piece * TOKENS, TOKENS)
            values[head, rows, :HD] = pairs[piece][head * 2 + 1]
            values[head, rows, HD:] = jnp.ones((TOKENS, HD), bf16)
    on_diagonal = diagonal()
    parts = [(piece, half) for piece in range(SIDE) for half in range(TOKENS // TILE)]
    tiles = range(HEADS * TOKENS // TILE)
    tops = []
    for tile in tiles:
        head = tile * TILE // TOKENS
        query = queries[tile * TILE : (tile + 1) * TILE, :]
        highest = None
        for index, (piece, half) in enumerate(parts):
            part = lax.dot_general(
                query,
                pairs[piece][head * 2, half * TILE : (half + 1) * TILE, :],
                (((1,), (1,)), ((), ())),
                preferred_element_type=f32,
            )
            scores[tile, :, index * TILE : (index + 1) * TILE] = part
            here = jnp.maximum(part[:, :HD], part[:, HD:])
            highest = here if highest is None else jnp.maximum(highest, here)
        tops.append(jnp.max(highest, axis=1, keepdims=True) * score_scale)
    for tile in tiles:
        for index in range(len(parts)):
            columns = slice(index * TILE, (index + 1) * TILE)
            part = scores[tile, :, columns]
            weights[tile, :, columns] = jnp.exp2(part * score_scale - tops[tile]).astype(bf16)
    for tile in tiles:
        total = jnp.dot(
            weights[tile], values[tile * TILE // TOKENS], preferred_element_type=f32
        )
        weight_sum = total[:, HD:]
        out[tile * TILE : (tile + 1) * TILE, :] = (total[:, :HD] / weight_sum).astype(bf16)
        level = tops[tile] + jnp.log2(weight_sum)
        for part in range(TILE // HD):
            block = level[part * HD : (part + 1) * HD, :]
            row = jnp.sum(jnp.where(on_diagonal, block, 0.0), axis=0, keepdims=True)
            stats[tile * (TILE // HD) + part : tile * (TILE // HD) + part + 1, :] = row
    level = stats[...]
    high = level.astype(bf16).astype(f32)
    middle = (level - high).astype(bf16).astype(f32)
    low = level - high - middle
    block = jnp.concatenate([high, middle, low, jnp.zeros_like(low)], axis=0)
    out[HEADS * TOKENS :, :] = block.astype(bf16)


def terms(value):
    high = value.astype(bf16)
    low = (value - high.astype(f32)).astype(bf16)
    return jnp.concatenate([high, low], axis=0)


def term_dot(value, weight):
    both = jnp.dot(terms(value), weight, preferred_element_type=f32)
    return both[: value.shape[0]] + both[value.shape[0] :]


def prepare_kernel(
    step, place, main_mod, guide_mod, main_head, guide_head, weights, scales, means, shifts
):
    zh, core, zl = place[0], place[1], place[2]
    first = pl.ds(pl.multiple_of((zl * 5 + 2 * zh + core) * HD, HD), HD)
    shared = pl.ds(pl.multiple_of((zl * 5 + 4) * HD, HD), HD)
    guide = pl.ds(pl.multiple_of((zl * 2 + zh) * HD, HD), HD)
    weights[0] = main_head[first, :]
    scales[...] = jnp.zeros_like(scales)
    scales[0:1, :] = 1.0 + main_mod[0, :, first][1:2].astype(f32)

    @pl.when(core == 0)
    def _():
        weights[1] = guide_head[guide, :]
        scales[1:2, :] = 1.0 + guide_mod[0, :, guide][1:2].astype(f32)

    @pl.when(core == 1)
    def _():
        weights[1] = main_head[shared, :]
        scales[1:2, :] = 1.0 + main_mod[0, :, shared][1:2].astype(f32)

    def rows_of(table, order):
        both = table[0].astype(f32)
        shift, scale = both[0:1], 1.0 + both[1:2]
        owner = lax.broadcasted_iota(jnp.int32, scale.shape, 1) >> 7
        rows = [jnp.where(owner == head, scale, 0.0) for head in order] + [shift]
        rows += [jnp.zeros_like(shift)] * (-len(rows) % 8)
        return jnp.concatenate(rows, axis=0)

    main_order = [
        zl * 5 + 2 * zh + core for core in range(CORE) for zh in range(ZH) for zl in range(ZL)
    ] + [zl * 5 + 4 for zl in range(ZL)]
    guide_order = [zl * 2 + zh for zh in range(ZH) for zl in range(ZL)]
    main_rows = term_dot(rows_of(main_mod, main_order), main_head[...])
    guide_rows = term_dot(rows_of(guide_mod, guide_order), guide_head[...])
    main_rows = jnp.concatenate([main_rows, jnp.zeros_like(main_rows)], axis=1)
    guide_rows = jnp.concatenate([jnp.zeros_like(guide_rows), guide_rows], axis=1)
    means[...] = jnp.zeros_like(means)
    for source in range(CORE * Z):
        means[source * 8 : source * 8 + 1, :] = main_rows[source : source + 1]
    for source in range(Z):
        means[source * 8 + 4 : source * 8 + 5, :] = guide_rows[source : source + 1]
        at = (Z + source) * 8 + 4
        means[at : at + 1, :] = main_rows[2 * Z + source % ZL : 2 * Z + source % ZL + 1]
    shifts[...] = jnp.zeros_like(shifts)
    shifts[0:1, :] = main_rows[20:21] + guide_rows[8:9]


def levels_of(part):
    block = part[HEADS * TOKENS :, :].astype(f32)
    return block[0:8] + block[8:16] + block[16:24]


def merge(parts, levels):
    top = levels[0]
    for level in levels[1:]:
        top = jnp.maximum(top, level)
    shares = [jnp.exp2(level - top) for level in levels]
    whole = sum(shares)
    filler = jnp.zeros((HD - 8, HD), f32)
    shares = [jnp.transpose(jnp.concatenate([share / whole, filler], axis=0)) for share in shares]
    tiles = []
    for tile in range(HEADS * TOKENS // HD):
        rows = slice(tile * HD, (tile + 1) * HD)
        tiles.append(
            sum(
                part[rows, :].astype(f32) * share[:, tile : tile + 1]
                for part, share in zip(parts, shares)
            )
        )
    return tiles, top + jnp.log2(whole)


def merge_kernel(*refs):
    parts, result, level = refs[:-2], refs[-2], refs[-1]
    tiles, level[...] = merge(parts, [levels_of(part) for part in parts])
    for tile, value in enumerate(tiles):
        result[tile * HD : (tile + 1) * HD, :] = value


def combine_kernel(place, weights, scales, former, former_level, part, send):
    on_diagonal = diagonal()
    tiles, unused = merge([former, part], [former_level[...], levels_of(part)])
    blocks = TOKENS // HD
    for tile in range(blocks):
        narrow = tiles[blocks + tile // ZH]
        start = tile % ZH * (HD // ZH)
        pieces = []
        for row in range(start, start + HD // ZH, PART):
            pieces += [narrow[row : row + PART]] * ZH
        wide = jnp.concatenate(pieces, axis=0)
        tiles.append(jnp.where(place[1] == 1, wide, tiles[blocks + tile]))
    tiles = tiles[:blocks] + tiles[2 * blocks :]
    flows, stats = [], []
    for head in range(HEADS):
        attended = jnp.concatenate(tiles[head * blocks : (head + 1) * blocks], axis=0).astype(bf16)
        mean = jnp.mean(attended.astype(f32), axis=1, keepdims=True)
        centered = attended.astype(f32) - mean
        square = jnp.sum(centered * centered, axis=1, keepdims=True)
        flow = term_dot(centered * scales[head : head + 1, :], weights[head]).astype(bf16)
        for tile in range(blocks):
            rows = slice(tile * HD, (tile + 1) * HD)
            flows.append(flow[rows])
            both = [
                jnp.sum(jnp.where(on_diagonal, value[rows], 0.0), axis=0, keepdims=True)
                for value in (mean, square)
            ]
            both = jnp.concatenate(both, axis=0)
            high = both.astype(bf16).astype(f32)
            middle = (both - high).astype(bf16).astype(f32)
            stats.append((jnp.concatenate([high, middle], axis=0), both - high - middle))

    gap = jnp.zeros((2, HD), f32)
    for tile in range(blocks):
        other = blocks + tile
        rows = jnp.concatenate([flows[tile], flows[other]], axis=1)
        both = jnp.concatenate(
            [stats[tile][0], stats[other][0], stats[tile][1], gap, stats[other][1], gap],
            axis=0,
        ).astype(bf16)
        for zl in range(ZL):
            send[tile * ZL + zl, 0:ROWS, :] = rows[zl * ROWS : (zl + 1) * ROWS, :]
            send[tile * ZL + zl, ROWS : ROWS + 16, :] = both


def sigma_at(index):
    remaining = 1.0 - index.astype(f32) / STEPS
    return flow_shift * remaining / (1.0 + (flow_shift - 1.0) * remaining)


def final_kernel(step, place, got, means, shifts, latents, velocity, advanced, columns):
    zl = place[2]

    def flows(source):
        return got[source, 0:ROWS, :].astype(f32)

    lower = sum(flows(source) for source in range(Z))
    upper = sum(flows(Z + source) for source in range(Z))
    shared = [sum(flows(Z + zh * ZL + zl) for zl in range(ZL)) for zh in range(ZH)]
    shared = jnp.concatenate([shared[0][:PART], shared[1][PART:]], axis=0)
    upper = upper[:, :C] + shared[:, C:]
    total = lower + jnp.concatenate([upper, jnp.zeros((ROWS, C), f32)], axis=1)

    table = []
    for source in range(CORE * Z):
        block = got[source, ROWS : ROWS + 16, :].astype(f32)
        high = block[:8]
        table.append(high + jnp.concatenate([high[2:], high[:2]], axis=0) + block[8:])
    table = jnp.concatenate(table, axis=0)
    row = lax.broadcasted_iota(jnp.int32, (HD, HD), 0)
    kind, source = row & 7, row >> 3
    token = lax.broadcasted_iota(jnp.int32, (HD, HD), 1)
    second = (source >= Z) & (((source - Z) >> 2) == ((token >> 4) & 1))

    def gathered(count, of_mean, of_square):
        mean = jnp.sum(jnp.where(of_mean, table, 0.0), axis=0, keepdims=True) / count
        apart = jnp.where(of_mean, table - mean, 0.0)
        spread = jnp.where(of_square, table, 0.0) + HD * (apart * apart)
        spread = jnp.sum(spread, axis=0, keepdims=True) / (count * HD)
        return apart, lax.rsqrt(spread + epsilon)

    main, main_shrink = gathered(
        20, (kind == 0) | ((kind == 4) & second), (kind == 1) | ((kind == 5) & second)
    )
    guide, guide_shrink = gathered(8, (kind == 4) & (source < Z), (kind == 5) & (source < Z))
    block = main + guide
    block = jnp.where(row == 2, main_shrink, jnp.where(row == 3, guide_shrink, block))
    columns[...] = jnp.transpose(block)
    mine = columns[pl.ds(pl.multiple_of(zl * ROWS, ROWS), ROWS), :]
    lane = lax.broadcasted_iota(jnp.int32, (ROWS, HD), 1)
    shrink = jnp.where(lane < C, mine[:, 2:3], mine[:, 3:4])
    high = means[...].astype(bf16)
    low = (means[...] - high.astype(f32)).astype(bf16)
    both = jnp.concatenate([high, low], axis=1)
    moved = jnp.dot(terms(mine), both, preferred_element_type=f32)
    moved = moved[:ROWS, :HD] + moved[ROWS:, :HD] + moved[:ROWS, HD:]
    flow = shrink * (total + moved) + shifts[0:1, :]
    main_flow, guide_flow = flow[:, :C], flow[:, C:]
    result = guide_flow + guidance * (main_flow - guide_flow)
    now = jnp.full((1, 1), step[0], jnp.int32)
    velocity[0] = result
    advanced[0] = latents[0] + (sigma_at(now + 1) - sigma_at(now)) * result


def plane_shift(array, by, axis_of_core):
    pairs = []
    for x in range(X):
        for y in range(Y):
            for core in range(CORE):
                if axis_of_core[core] == "x":
                    to = ((x + by) % X, y)
                else:
                    to = (x, (y + by) % Y)
                pairs.append(((x * Y + y) * CORE + core, (to[0] * Y + to[1]) * CORE + core))
    return lax.ppermute(array, ("x", "y", "core"), pairs)


SHIFTS = (-1, 1, 2)


def attend(queries, pairs):
    rows, tiles = HEADS * TOKENS, HEADS * TOKENS // TILE
    return pl.pallas_call(
        attend_kernel,
        out_shape=shape(rows + STAT, HD),
        in_specs=[VMEM] * (1 + SIDE),
        out_specs=VMEM,
        scratch_shapes=[
            pltpu.VMEM((HEADS, KEYS, 2 * HD), bf16),
            pltpu.VMEM((tiles, TILE, KEYS), f32),
            pltpu.VMEM((tiles, TILE, KEYS), bf16),
            pltpu.VMEM((8, HD), f32),
        ],
        compiler_params=params(32),
        cost_estimate=pl.CostEstimate(
            flops=4 * rows * KEYS * HD,
            bytes_accessed=4 * HEADS * KEYS * HD,
            transcendentals=rows * KEYS,
        ),
        name="attend",
    )(queries, *pairs)


def on_device(
    main_query,
    main_key,
    main_value,
    guide_query,
    guide_key,
    guide_value,
    latents,
    step_index,
    main_mod,
    guide_mod,
    main_head,
    guide_head,
):
    place = jnp.stack([lax.axis_index(name) for name in ("zh", "core", "zl")]).astype(jnp.int32)
    guide_send, guide_own = pl.pallas_call(
        pack_guide_kernel,
        out_shape=(shape(3, BLOCK, HD),) * 2,
        in_specs=[SMEM] + [ANY] * 3,
        out_specs=(VMEM,) * 2,
        scratch_shapes=[pltpu.SemaphoreType.DMA((6,))],
        compiler_params=params(16),
        name="pack_guide",
    )(place, guide_query, guide_key, guide_value)
    send = pl.pallas_call(
        pack_kernel,
        out_shape=shape(Z, MESSAGE, HD),
        in_specs=[ANY] * 3,
        out_specs=VMEM,
        scratch_shapes=[
            pltpu.VMEM((3, ROWS, 20 * HD), bf16),
            pltpu.SemaphoreType.DMA((3,)),
        ],
        compiler_params=params(60),
        name="pack",
    )(main_query, main_key, main_value)
    whole = lambda *dims: pl.BlockSpec(dims, lambda i, step, place: (0,) * len(dims))
    row = lambda *dims: pl.BlockSpec(dims, lambda i, step, place: (step[0], 0, 0))
    weights, scales, means, shifts = pl.pallas_call(
        prepare_kernel,
        out_shape=(
            shape(HEADS, HD, C),
            shape(8, HD, dtype=f32),
            shape(HD, HD, dtype=f32),
            shape(8, HD, dtype=f32),
        ),
        grid_spec=pltpu.PrefetchScalarGridSpec(
            num_scalar_prefetch=2,
            grid=(1,),
            in_specs=[
                row(1, 2, 20 * HD),
                row(1, 2, 8 * HD),
                whole(20 * HD, C),
                whole(8 * HD, C),
            ],
            out_specs=[whole(HEADS, HD, C), whole(8, HD), whole(HD, HD), whole(8, HD)],
        ),
        compiler_params=params(16),
        name="prepare",
    )(step_index, place, main_mod, guide_mod, main_head, guide_head)
    halves = ("zh", "core")
    guide_core = lax.ppermute(guide_own, halves, [(1, 0), (3, 2)])
    guide_half = lax.ppermute(guide_send, halves, [(0, 2), (2, 0)])
    guide_across = lax.ppermute(guide_send, halves, [(1, 2), (3, 0)])
    got = lax.all_to_all(send, ("zh", "zl"), split_axis=0, concat_axis=0, tiled=True)
    got, guide_core, guide_half, guide_across, weights, scales, means, shifts = (
        lax.optimization_barrier(
            (got, guide_core, guide_half, guide_across, weights, scales, means, shifts)
        )
    )
    sibling = lax.ppermute(got, "core", [(0, 1), (1, 0)])
    queries, pairs = pl.pallas_call(
        unpack_kernel,
        out_shape=(shape(HEADS * TOKENS, HD), shape(2 * HEADS, TOKENS, HD)),
        in_specs=[SMEM] + [VMEM] * 6,
        out_specs=(VMEM,) * 2,
        compiler_params=params(16),
        name="unpack",
    )(place, got, sibling, guide_own, guide_core, guide_half, guide_across)
    all_queries = [queries] + [plane_shift(queries, by, "xy") for by in SHIFTS]
    all_pairs = [pairs] + [plane_shift(pairs, by, "yx") for by in SHIFTS]
    parts = [attend(q, all_pairs) for q in all_queries]
    parts[1:] = [plane_shift(p, -by, "xy") for p, by in zip(parts[1:], SHIFTS)]
    former, level = pl.pallas_call(
        merge_kernel,
        out_shape=(shape(HEADS * TOKENS, HD, dtype=f32), shape(8, HD, dtype=f32)),
        in_specs=[VMEM] * (SIDE - 1),
        out_specs=(VMEM,) * 2,
        compiler_params=params(16),
        name="merge",
    )(*parts[:-1])
    send = pl.pallas_call(
        combine_kernel,
        out_shape=shape(CORE * Z, ROWS + 16, HD),
        in_specs=[SMEM] + [VMEM] * 5,
        out_specs=VMEM,
        compiler_params=params(16),
        name="combine",
    )(place, weights, scales, former, level, parts[-1])
    got = lax.all_to_all(send, ("core", "zh", "zl"), split_axis=0, concat_axis=0, tiled=True)
    velocity, advanced = pl.pallas_call(
        final_kernel,
        out_shape=(shape(1, ROWS, C, dtype=f32),) * 2,
        in_specs=[SMEM] * 2 + [VMEM] * 4,
        out_specs=(VMEM,) * 2,
        scratch_shapes=[pltpu.VMEM((HD, HD), f32)],
        compiler_params=params(16),
        name="final",
    )(step_index, place, got, means, shifts, latents)
    return velocity, advanced


def solution(mesh):
    fine = Mesh(mesh.devices.reshape(ZL, X, Y, ZH, CORE), ("zl", "x", "y", "zh", "core"))
    seq = ("x", "y", "zh", "core")
    return jax.shard_map(
        on_device,
        mesh=fine,
        in_specs=(P(seq, "zl", None),) * 3
        + (P(seq, None, "zl"),) * 3
        + (P(seq, "zl", None),)
        + (P(),) * 5,
        out_specs=(P(seq, "zl", None),) * 2,
        check_vma=False,
    )
```
